128 devices in a mesh: tm: 4 (over y_lo, core), space: 32 (over x, z, y_hi).
Axes of the slice: x: 4, y: 4 (y_hi: 2, y_lo: 2; y = y_hi * 2 + y_lo), z: 4, core: 2. Of those that a mesh axis runs over, the one named last changes fastest.
Arguments:
- departures: float32 [8, 32, 256, 512], P('tm', None, 'space'), may hold values from -6 to 6
- innovations: float32 [524288], P(('tm', 'space')), may hold values from -6 to 6
- obs_variance: float32 [524288], P(('tm', 'space')), may hold values from 0.5 to 2
- dual_state: float32 [8, 32, 256, 512], P('tm', None, 'space'), may hold values from -6 to 6
- obs_dual: float32 [524288], P(('tm', 'space')), may hold values from -6 to 6
- increment: float32 [8, 32, 256, 512], P('tm', None, 'space'), may hold values from -6 to 6
- trajectory: float32 [8, 32, 256, 512], P('tm', None, 'space'), may hold values from -6 to 6
- lat_mix: float32 [256, 256], replicated, may hold values from -0.375 to 0.375
- spectrum: float32 [257], replicated, may hold values from 0.1 to 1
- error_scale: float32 [8], P('tm'), may hold values from 0.3 to 1
- obs_time: int32 [524288], P(('tm', 'space')), may hold values from 0 to 7, as said below
- obs_level: int32 [524288], P(('tm', 'space')), may hold values from 0 to 31
- obs_point: int32 [524288], P(('tm', 'space')), may hold values from 0 to 131071, as said below
Outputs:
- dual_next: float32 [8, 32, 256, 512], P('tm', None, 'space')
- obs_dual_next: float32 [524288], P(('tm', 'space'))
- increment_next: float32 [8, 32, 256, 512], P('tm', None, 'space')
- trajectory_next: float32 [8, 32, 256, 512], P('tm', None, 'space')
The draws below stay inside these ranges and needn't reach their ends.
Inputs may be any that keep to these rules, and one draw needn't show every extreme that they name: `obs_time`: observations come in blocks of 4096; block b lies in the sub-windows (b // number of latitude bands) * 2 to that plus 2 - 1. `obs_point`: block b of 4096 observations lies in the latitudes (b mod number of latitude bands) * 8 to that plus 8 - 1.
All inputs are finite; a program needn't handle non-finite values.
Results may differ from the reference program's by a relative error of at most 0.0001.
Values sent between devices are 32-bit elements; how exact they have to be, the bound alone decides.
A program may use at most 128 MiB of HBM per device.

```python
import math
import jax
import jax.numpy as jnp
from jax import lax

LEV = 32
LAT_DEV = 8
NLON = 512
SW_DEV = 2
ITERS = 2
OBS_DEV = 4096
SUBWIN = 8
NLAT = 256
NOBS = 524288
N_SPACE = 32


def draw_obs_time(key, part):
    key = jax.random.fold_in(key, 11)
    order = jnp.arange(NOBS, dtype=jnp.int32)
    block = order // OBS_DEV
    group = block // N_SPACE
    inner = order % OBS_DEV
    window = jax.random.randint(key, (NOBS,), 0, SW_DEV, dtype=jnp.int32)
    window = jnp.where(inner == 0, SW_DEV - 1, jnp.where(inner == 1, 0, window))
    return (group * SW_DEV + window).astype(jnp.int32)


def draw_obs_point(key, part):
    key = jax.random.fold_in(key, 23)
    first_key, second_key = jax.random.split(key)
    order = jnp.arange(NOBS, dtype=jnp.int32)
    band = order // OBS_DEV % N_SPACE
    inner = order % OBS_DEV
    row_pick = jax.random.randint(first_key, (NOBS,), 0, LAT_DEV, dtype=jnp.int32)
    column = jax.random.randint(second_key, (NOBS,), 0, NLON, dtype=jnp.int32)
    row_pick = jnp.where(inner == 0, 0, jnp.where(inner == 1, LAT_DEV - 1, row_pick))
    column = jnp.where(inner == 0, 0, jnp.where(inner == 1, NLON - 1, column))
    return ((band * LAT_DEV + row_pick) * NLON + column).astype(jnp.int32)


def with_ends(entries, rng, low, high):
    longest = entries.shape.index(max(entries.shape))
    spots = []
    for shift in (0, 1):
        where = [jax.random.randint(jax.random.fold_in(rng, axis), (), 0, length) for axis, length in enumerate(entries.shape)]
        where[longest] = (where[longest] + shift) % entries.shape[longest]
        spots.append(tuple(where))
    return entries.at[spots[0]].set(low).at[spots[1]].set(high)


def steps_of(own_key, extent, shards, low, high):
    def one(position, shards_of):
        draws = jax.random.uniform(jax.random.fold_in(jax.random.fold_in(own_key, 6), position), (shards_of,), jnp.float32, low / len(shards), high / len(shards))
        return jnp.repeat(jnp.exp(draws), extent[position] // shards_of).reshape((-1,) + (1,) * (len(extent) - position - 1))

    level = one(*shards[0])
    for cut in shards[1:]:
        level = level * one(*cut)
    return level


def centred(stream_key, shape, width, limit, pieces=(), kind=jnp.bfloat16):
    result = width * jax.random.normal(stream_key, shape, jnp.float32)
    if pieces:
        result = result * steps_of(stream_key, shape, pieces, -0.22, 0.18)
    return jnp.clip(result, -limit, limit).astype(kind)


def setup_inputs(seed: int = 0) -> dict:
    keys = jax.random.split(jax.random.key(seed), 14)
    return {
        "departures": centred(keys[0], (SUBWIN, LEV, NLAT, NLON), 1.0, 6.0, ((0, 4), (2, 32)), jnp.float32),
        "innovations": centred(keys[1], (NOBS,), 1.0, 6.0, ((0, 128),), jnp.float32),
        "obs_variance": jnp.clip(jnp.exp(math.log(2.0) - 1.3862944 * jax.random.uniform(keys[2], (NOBS,), jnp.float32) ** steps_of(keys[2], (NOBS,), ((0, 128),), -0.2, 0.2)), 0.5, 2.0),
        "dual_state": centred(keys[3], (SUBWIN, LEV, NLAT, NLON), 1.0, 6.0, ((0, 4), (2, 32)), jnp.float32),
        "obs_dual": centred(keys[4], (NOBS,), 1.0, 6.0, ((0, 128),), jnp.float32),
        "increment": centred(keys[5], (SUBWIN, LEV, NLAT, NLON), 1.0, 6.0, ((0, 4), (2, 32)), jnp.float32),
        "trajectory": centred(keys[6], (SUBWIN, LEV, NLAT, NLON), 1.0, 6.0, ((0, 4), (2, 32)), jnp.float32),
        "lat_mix": centred(keys[7], (NLAT, NLAT), NLAT ** -0.5, 0.375, (), jnp.float32),
        "spectrum": jnp.clip(jnp.exp(jax.random.uniform(keys[8], (NLON // 2 + 1,), jnp.float32, math.log(0.1), math.log(1.0))), 0.1, 1.0),
        "error_scale": jnp.clip(jnp.exp(math.log(1.0) - 1.2039728 * jax.random.uniform(keys[9], (SUBWIN,), jnp.float32) ** steps_of(keys[9], (SUBWIN,), ((0, 4),), -0.2, 0.2)), 0.3, 1.0),
        "obs_time": draw_obs_time(jax.random.fold_in(keys[13], 71), 0),
        "obs_level": with_ends(jax.random.randint(keys[11], (NOBS,), 0, LEV), jax.random.fold_in(keys[11], 1), 0, LEV - 1).astype(jnp.int32),
        "obs_point": draw_obs_point(jax.random.fold_in(keys[13], 71), 0),
    }


diffusion = 0.1

def winds(trajectory):
    return (0.5 * jnp.tanh(trajectory), 0.5 * jnp.sin(trajectory))

def advance(field, trajectory):
    toward_east, toward_north = winds(trajectory)
    eastern = jnp.roll(field, -1, axis=-1)
    western = jnp.roll(field, 1, axis=-1)
    padded = jnp.pad(field, ((0, 0), (1, 1), (0, 0)))
    northern = padded[:, 2:, :]
    southern = padded[:, :-2, :]
    return field - 0.5 * toward_east * (eastern - western) - 0.5 * toward_north * (northern - southern) + diffusion * (eastern + western + northern + southern - 4.0 * field)

def adjoint(field, trajectory):
    _, pull = jax.vjp(lambda values: advance(values, trajectory), field)
    return pull(field)[0]

def forward_l(increment, trajectory):
    previous = jnp.concatenate([jnp.zeros_like(increment[:1]), increment[:-1]], 0)
    moved = lax.map(lambda member: advance(member[0], member[1]), (previous, trajectory))
    return increment - moved

def backward_l(dual, trajectory):
    pulled = lax.map(lambda member: adjoint(member[0], member[1]), (dual, trajectory))
    following = jnp.concatenate([pulled[1:], jnp.zeros_like(pulled[:1])], 0)
    return dual - following

def cover(field, lat_mix, spectrum, error_scale):

    def single(member):
        piece, scale = member
        smooth = jnp.fft.irfft(jnp.fft.rfft(piece, axis=-1) * spectrum, n=NLON, axis=-1)
        mixed = smooth + jnp.einsum('ab,lbc->lac', lat_mix, smooth, precision=lax.Precision.HIGHEST)
        return mixed * (scale * scale)
    return lax.map(single, (field, error_scale))

def reference(departures, innovations, obs_variance, dual_state, obs_dual, increment, trajectory, lat_mix, spectrum, error_scale, obs_time, obs_level, obs_point):
    latitude = obs_point // NLON
    longitude = obs_point % NLON
    for iteration in range(ITERS):
        lx_term = forward_l(increment, trajectory)
        ltl_term = backward_l(dual_state, trajectory)
        seen = increment[obs_time, obs_level, latitude, longitude]
        spread_back = jnp.zeros_like(increment).at[obs_time, obs_level, latitude, longitude].add(obs_dual)
        r_state = departures - cover(dual_state, lat_mix, spectrum, error_scale) - lx_term
        r_obs = innovations - obs_variance * obs_dual - seen
        r_dual = -ltl_term - spread_back
        dual_state = dual_state + r_dual
        obs_dual = obs_dual + r_obs / obs_variance
        increment = increment + r_state - cover(r_dual, lat_mix, spectrum, error_scale)
    analysis = trajectory + increment
    choose = jnp.minimum(jnp.arange(SUBWIN, dtype=jnp.int32) + SW_DEV, SUBWIN - 1)
    return (dual_state, obs_dual, increment, analysis[choose])
```

```python
import math

import jax
import jax.numpy as jnp
import numpy as np
from jax import lax
from jax.sharding import PartitionSpec as P

LAT_DEV = 8
NLON = 512
SW_DEV = 2
ITERS = 2

diffusion = 0.1


def shifted(block, axis, distance):
    devices = range(lax.axis_size(axis))
    route = [(i - distance, i) for i in devices if i - distance in devices]
    return lax.ppermute(block, axis, route)


def circulant(spectrum, width):
    modes = np.arange(width // 2 + 1)
    cells = np.arange(width)
    angle = (cells[:, None] * modes[None, :] % width) * (2.0 * math.pi / width)
    factor = jnp.asarray(np.where((modes == 0) | (modes == width // 2), 1.0, 2.0).astype(np.float32) / width) * spectrum
    cosine = jnp.asarray(np.cos(angle).astype(np.float32))
    sine = jnp.asarray(np.sin(angle).astype(np.float32))
    left = jnp.concatenate([cosine * factor, sine * factor], axis=1)
    right = jnp.concatenate([cosine, sine], axis=1)
    return jnp.dot(left, right.T, precision=lax.Precision.HIGHEST)


def halo(up, down):
    return shifted(up, "space", 1), shifted(down, "space", -1)


def advance_local(field, east, north):
    below, above = halo(field[:, :, -1:], field[:, :, :1])
    padded = jnp.concatenate([below, field, above], axis=2)
    return (
        0.6 * field
        + jnp.roll(field, -1, axis=3) * (0.2 - east)
        + jnp.roll(field, 1, axis=3) * east
        + padded[:, :, 2:] * (0.2 - north)
        + padded[:, :, :-2] * north
    )


def adjoint_local(field, east, north):
    toward_south = field * north
    toward_north = field * (0.2 - north)
    below, above = halo(toward_north[:, :, -1:], toward_south[:, :, :1])
    return (
        0.6 * field
        + jnp.roll(field * east, -1, axis=3)
        + jnp.roll(field * (0.2 - east), 1, axis=3)
        + jnp.concatenate([toward_south[:, :, 1:], above], axis=2)
        + jnp.concatenate([below, toward_north[:, :, :-1]], axis=2)
    )


def cover(field, zonal, lat_mix, scale):
    bands = lax.axis_size("space")
    windows, levels, rows, width = field.shape
    whole = lax.all_to_all(field, "space", split_axis=1, concat_axis=2, tiled=True)
    whole = whole.reshape(windows, bands * rows, width)
    smooth = jnp.einsum("sax,xy->say", whole, zonal, precision=lax.Precision.HIGH)
    mixed = smooth + jnp.einsum("ab,sby->say", lat_mix, smooth, precision=lax.Precision.HIGH)
    mixed = (mixed * (scale * scale)[:, None, None]).reshape(windows, 1, bands * rows, width)
    return lax.all_to_all(mixed, "space", split_axis=2, concat_axis=1, tiled=True)


def halves(values):
    high = lax.reduce_precision(values, 8, 7)
    return high.astype(jnp.bfloat16), (values - high).astype(jnp.bfloat16)


def on_device(
    departures,
    innovations,
    obs_variance,
    dual_state,
    obs_dual,
    increment,
    trajectory,
    lat_mix,
    spectrum,
    error_scale,
    obs_time,
    obs_level,
    obs_point,
):
    group = lax.axis_index("tm")
    band = lax.axis_index("space")
    zonal = circulant(spectrum, NLON)
    east = 0.1 + 0.25 * jnp.tanh(trajectory)
    north = 0.1 + 0.25 * jnp.sin(trajectory)
    state_shape = increment.shape
    levels = state_shape[1]
    row_count = state_shape[0] * state_shape[1] * state_shape[2]
    window = obs_time - group * SW_DEV
    latitude = obs_point // NLON - band * LAT_DEV
    longitude = obs_point % NLON
    row_index = (window * levels + obs_level) * state_shape[2] + latitude
    row_hit = jnp.arange(row_count, dtype=jnp.int32)[:, None] == row_index[None, :]
    row_table = row_hit.astype(jnp.bfloat16)
    column_hit = jnp.arange(NLON, dtype=jnp.int32)[:, None] == longitude[None, :]

    def observe(state):
        high, low = halves(state.reshape(row_count, NLON))
        dims = (((0,), (0,)), ((), ()))
        picked = lax.dot_general(high, row_table, dims, preferred_element_type=jnp.float32)
        picked = picked + lax.dot_general(low, row_table, dims, preferred_element_type=jnp.float32)
        return jnp.sum(jnp.where(column_hit, picked, 0.0), axis=0)

    def spread(values):
        dims = (((1,), (1,)), ((), ()))
        parts = [
            lax.dot_general(
                row_table,
                jnp.where(column_hit, part[None, :], jnp.bfloat16(0)),
                dims,
                preferred_element_type=jnp.float32,
            )
            for part in halves(values)
        ]
        return (parts[0] + parts[1]).reshape(state_shape)

    for iteration in range(ITERS):
        last_prev = shifted(increment[-1:], "tm", 1)
        previous = jnp.concatenate([last_prev, increment[:-1]], 0)
        moved = advance_local(previous, east, north)
        pulled = adjoint_local(dual_state, east, north)
        first_next = shifted(pulled[:1], "tm", -1)
        dual_state = jnp.concatenate([pulled[1:], first_next], 0) - spread(obs_dual)
        r_obs = innovations - obs_variance * obs_dual - observe(increment)
        increment = departures + moved - cover(dual_state, zonal, lat_mix, error_scale)
        obs_dual = obs_dual + r_obs / obs_variance
    analysis = trajectory + increment
    slid = shifted(analysis, "tm", -1)
    is_last = group == lax.axis_size("tm") - 1
    slid = jnp.where(is_last, jnp.broadcast_to(analysis[-1:], slid.shape), slid)
    return (dual_state, obs_dual, increment, slid)


def solution(mesh):
    state = P("tm", None, "space", None)
    flat = P(("tm", "space"))
    placed = (state, flat, flat, state, flat, state, state, P(), P(), P("tm"), flat, flat, flat)
    return jax.shard_map(
        on_device,
        mesh=mesh,
        in_specs=placed,
        out_specs=(state, flat, state, state),
        check_vma=False,
    )
```

```python
import functools
import math

import jax
import jax.numpy as jnp
import numpy as np
from jax import lax
from jax.experimental import pallas as pl
from jax.experimental.pallas import tpu as pltpu
from jax.sharding import PartitionSpec as P

MESH = pl.DeviceIdType.MESH
ROWS = 8
GROUP = 4
F32 = jnp.float32
BF16 = jnp.bfloat16
SINE = (-2.5052108385e-8, 2.7557319224e-6, -1.9841269841e-4, 8.3333333333e-3, -1.6666666667e-1)


def sine(angle):
    turns = jnp.floor(angle * (1.0 / math.pi) + 0.5)
    rest = angle - turns * 3.140625
    rest = rest - turns * 9.67653589793e-4
    square = rest * rest
    series = SINE[0]
    for factor in SINE[1:]:
        series = series * square + factor
    half = turns * 0.5
    sign = 1.0 - 4.0 * (half - jnp.floor(half))
    return sign * (rest + rest * square * series)


def split(values):
    high = values.astype(BF16)
    return high, (values - high.astype(F32)).astype(BF16)


def dot(left, right, dims=((1,), (0,))):
    return lax.dot_general(left, right, (dims, ((), ())), preferred_element_type=F32)


def kernel(
    groups,
    bands,
    base_ref,
    mix_ref,
    scale_ref,
    dep,
    dual,
    incr,
    traj,
    innov,
    variance,
    held,
    time_ref,
    level_ref,
    point_ref,
    out_dual,
    out_held,
    out_incr,
    out_slid,
    east,
    north,
    zonal_hi,
    zonal_lo,
    mix_hi,
    mix_lo,
    row_ref,
    lon_ref,
    row_table,
    spread_ref,
    turned_hi,
    turned_lo,
    held1,
    dual1,
    pulled,
    pull_send,
    pull_recv,
    prior,
    incr1,
    part,
    slid_send,
    fore1,
    fore2,
    mixed1,
    mixed2,
    back1,
    back2,
    halo_send,
    halo_recv,
    far_send,
    far_recv,
    pull_ssem,
    pull_rsem,
    prior_ssem,
    prior_rsem,
    slid_ssem,
    slid_rsem,
    halo_ssem,
    halo_rsem,
):
    windows, levels, _, width = dep.shape
    obs = innov.shape[1]
    cells = windows * levels * ROWS
    chunk = min(512, obs)
    me = lax.axis_index("space")
    grp = lax.axis_index("tm")
    has_prev, has_next = grp > 0, grp < groups - 1
    has_below, has_above = me > 0, me < bands - 1
    line = lax.broadcasted_iota(jnp.int32, (ROWS, width), 0)
    is_first, is_last = line == 0, line == ROWS - 1

    def both(*flags):
        return functools.reduce(jnp.logical_and, flags)

    barrier = pltpu.get_barrier_semaphore()
    around = ((0, None), (-1, has_below), (1, has_above))

    def greet(j, carry):
        pl.semaphore_signal(barrier, inc=1, device_id=(grp, lax.rem(me + j, bands)), device_id_type=MESH)
        return carry

    lax.fori_loop(1, bands, greet, 0)
    for shift, there in ((-1, has_prev), (1, has_next)):
        for step, beside in around:
            flags = [there] if beside is None else [there, beside]

            @pl.when(both(*flags))
            def _(shift=shift, step=step):
                pl.semaphore_signal(barrier, inc=1, device_id=(grp + shift, me + step), device_id_type=MESH)

    def await_barrier():
        beside = 1 + has_below.astype(jnp.int32) + has_above.astype(jnp.int32)
        other = has_prev.astype(jnp.int32) + has_next.astype(jnp.int32)
        pl.semaphore_wait(barrier, bands - 1 + other * beside)

    def remote(source, target, ssem, rsem, device):
        return pltpu.make_async_remote_copy(
            src_ref=source, dst_ref=target, send_sem=ssem, recv_sem=rsem, device_id=device, device_id_type=MESH
        )

    def each_level(body):
        def step(i, carry):
            for u in range(GROUP):
                body(i * GROUP + u)
            return carry

        lax.fori_loop(0, levels // GROUP, step, 0)

    def rows_of(j):
        return pl.ds(pl.multiple_of(j * ROWS, ROWS), ROWS)

    def send_out(source, target, k, s):
        def step(j, carry):
            to = lax.rem(me + j, bands)
            remote(source.at[s, to], target.at[s, rows_of(me)], far_send.at[k, s], far_recv.at[k, s], (grp, to)).start()
            return carry

        lax.fori_loop(1, bands, step, 0)
        target[s, rows_of(me), :] = source[s, me]

    def send_back(source, target, k, s):
        def step(j, carry):
            to = lax.rem(me + j, bands)
            remote(source.at[s, rows_of(to)], target.at[s, me], far_send.at[k, s], far_recv.at[k, s], (grp, to)).start()
            return carry

        lax.fori_loop(1, bands, step, 0)
        target[s, me] = source[s, rows_of(me), :]

    def all_but_one(ref, s):
        return ref.at[s, pl.ds(0, bands - 1)] if ref.ndim == 4 else ref.at[s, pl.ds(0, (bands - 1) * ROWS)]

    def far_copy(source, target, k, s):
        return remote(all_but_one(source, s), all_but_one(target, s), far_send.at[k, s], far_recv.at[k, s], (grp, me))

    def halo(phase, way, s):
        pulls = phase < 2
        to_group = (grp - 1 if pulls else grp) if s == 0 else (grp if pulls else grp + 1)
        to_band = me + 1 if way == 0 else me - 1
        return remote(
            halo_send.at[phase, way, s],
            halo_recv.at[phase, way, 1 - s],
            halo_ssem.at[phase, way, s],
            halo_rsem.at[phase, way, 1 - s],
            (to_group, to_band),
        )

    def halo_sends(phase, way, s):
        beside = has_above if way == 0 else has_below
        if phase < 2 and s == 0:
            return both(beside, has_prev)
        if phase >= 2 and s == 1:
            return both(beside, has_next)
        return beside

    def halo_hears(phase, way, s):
        beside = has_below if way == 0 else has_above
        if phase < 2 and s == 1:
            return both(beside, has_next)
        if phase >= 2 and s == 0:
            return both(beside, has_prev)
        return beside

    def halo_start(phase, s):
        for way in (0, 1):

            @pl.when(halo_sends(phase, way, s))
            def _(way=way):
                halo(phase, way, s).start()

    def halo_wait(phase, s):
        for way in (0, 1):

            @pl.when(halo_hears(phase, way, s))
            def _(way=way):
                halo(phase, way, 1 - s).wait_recv()

            @pl.when(jnp.logical_not(halo_hears(phase, way, s)))
            def _(way=way):
                halo_recv[phase, way, s] = jnp.zeros((levels, width), F32)

    def halo_row(phase, way, s, lev):
        return halo_recv[phase, way, s, pl.ds(lev, 1), :]

    def pull_copy(k):
        return remote(pull_send.at[k], pull_recv.at[k], pull_ssem.at[k], pull_rsem.at[k], (grp - 1, me))

    def prior_copy(k, source):
        return remote(source.at[1], prior.at[k], prior_ssem.at[k], prior_rsem.at[k], (grp + 1, me))

    def hear_next(copy, buffer):
        @pl.when(has_next)
        def _():
            copy.wait_recv()

        @pl.when(jnp.logical_not(has_next))
        def _():
            buffer[...] = jnp.zeros(buffer.shape, F32)

    def hear_prev(copy, buffer):
        @pl.when(has_prev)
        def _():
            copy.wait_recv()

        @pl.when(jnp.logical_not(has_prev))
        def _():
            buffer[...] = jnp.zeros(buffer.shape, F32)

    def pull(phase, s, lev, field):
        pe, pn = east[s, lev], north[s, lev]
        down = field * pn
        up = field * (0.2 - pn)
        halo_send[phase, 0, s, pl.ds(lev, 1), :] = up[ROWS - 1 :, :]
        halo_send[phase, 1, s, pl.ds(lev, 1), :] = down[:1, :]
        return (
            0.6 * field
            + pltpu.roll(field * pe, width - 1, 1)
            + pltpu.roll(field * (0.2 - pe), 1, 1)
            + jnp.where(is_last, 0.0, pltpu.roll(down, ROWS - 1, 0))
            + jnp.where(is_first, 0.0, pltpu.roll(up, 1, 0))
        )

    def pulled_halo(phase, s, lev):
        return jnp.where(is_first, halo_row(phase, 0, s, lev), 0.0) + jnp.where(is_last, halo_row(phase, 1, s, lev), 0.0)

    def push(phase, s, lev, field):
        pe, pn = east[s, lev], north[s, lev]
        above = jnp.where(is_last, halo_row(phase, 1, s, lev), pltpu.roll(field, ROWS - 1, 0))
        below = jnp.where(is_first, halo_row(phase, 0, s, lev), pltpu.roll(field, 1, 0))
        return (
            0.6 * field
            + pltpu.roll(field, width - 1, 1) * (0.2 - pe)
            + pltpu.roll(field, 1, 1) * pe
            + above * (0.2 - pn)
            + below * pn
        )

    def edge_rows(phase, s, lev, field):
        halo_send[phase, 0, s, pl.ds(lev, 1), :] = field[ROWS - 1 :, :]
        halo_send[phase, 1, s, pl.ds(lev, 1), :] = field[:1, :]

    def piece(c):
        return pl.ds(pl.multiple_of(c * chunk, chunk), chunk)

    def tables():
        shift = width.bit_length() - 1
        point = point_ref[...]
        row_ref[...] = ((time_ref[...] - grp * windows) * levels + level_ref[...]) * ROWS + (
            lax.shift_right_logical(point, shift) - me * ROWS
        )
        lon_ref[...] = jnp.bitwise_and(point, width - 1)

        def step(c, carry):
            wanted = row_ref[:, piece(c)]
            block = 64
            for r in range(0, cells, block):
                spot = lax.broadcasted_iota(jnp.int32, (block, chunk), 0) + r
                row_table[r : r + block, piece(c)] = jnp.where(spot == wanted, 1.0, 0.0).astype(BF16)
            return carry

        lax.fori_loop(0, obs // chunk, step, 0)

    def spread(values):
        spread_ref[...] = jnp.zeros(spread_ref.shape, F32)

        def step(c, carry):
            weight = values[:, piece(c)]
            high = weight.astype(BF16).astype(F32)
            low = weight - high
            hit = lax.broadcasted_iota(jnp.int32, (width, chunk), 0) == lon_ref[:, piece(c)]
            chosen = row_table[:, piece(c)]
            total = dot(chosen, jnp.where(hit, high, 0.0).astype(BF16), ((1,), (1,)))
            total = total + dot(chosen, jnp.where(hit, low, 0.0).astype(BF16), ((1,), (1,)))
            spread_ref[...] += total
            return carry

        lax.fori_loop(0, obs // chunk, step, 0)

    def observe(state, old, new):
        turned = state[...].reshape(cells, width).T
        turned_hi[...], turned_lo[...] = split(turned)

        def step(c, carry):
            chosen = row_table[:, piece(c)]
            picked = dot(turned_hi[...], chosen) + dot(turned_lo[...], chosen)
            hit = lax.broadcasted_iota(jnp.int32, (width, chunk), 0) == lon_ref[:, piece(c)]
            seen = jnp.sum(jnp.where(hit, picked, 0.0), axis=0, keepdims=True)
            spread_of, before = variance[:, piece(c)], old[:, piece(c)]
            new[:, piece(c)] = before + (innov[:, piece(c)] - spread_of * before - seen) / spread_of
            return carry

        lax.fori_loop(0, obs // chunk, step, 0)

    def cover(source, target, s):
        high, low = split(source[s])
        smooth = dot(high, zonal_hi[...]) + (dot(high, zonal_lo[...]) + dot(low, zonal_hi[...]))
        high, low = split(smooth)
        mixed = smooth + (dot(mix_hi[...], high) + (dot(mix_hi[...], low) + dot(mix_lo[...], high)))
        scale = scale_ref[s]
        target[s] = mixed * (scale * scale)

    def first(lev):
        for s in (0, 1):
            wind = traj[s, lev]
            east[s, lev] = 0.1 + 0.25 * jnp.tanh(wind)
            north[s, lev] = 0.1 + 0.25 * sine(wind)
            value = pull(0, s, lev, dual[s, lev])
            if s == 0:
                pull_send[0, lev] = value
            else:
                pulled[lev] = value
            edge_rows(2, s, lev, incr[s, lev])

    each_level(first)
    await_barrier()

    @pl.when(has_prev)
    def _():
        pull_copy(0).start()

    for s in (1, 0):
        halo_start(0, s)

    @pl.when(has_next)
    def _():
        prior_copy(0, incr).start()

    for s in (0, 1):
        halo_start(2, s)

    tables()
    spread(held)

    def circulant(a, carry):
        tall = [pltpu.roll(base_ref[...], a * 16 + t, 1) for t in (0, 8)]
        high, low = split(jnp.concatenate(tall, axis=0))
        at = pl.ds(pl.multiple_of(a * 16, 16), 16)
        zonal_hi[at, :] = high
        zonal_lo[at, :] = low
        return carry

    halo_wait(0, 0)

    def dual1_here(lev):
        field = pulled[lev] + pulled_halo(0, 0, lev) - spread_ref[rows_of(lev), :]
        dual1[0, lev] = field
        pull_send[1, lev] = pull(1, 0, lev, field)

    each_level(dual1_here)
    send_out(dual1, fore1, 0, 0)

    @pl.when(has_prev)
    def _():
        pull_copy(1).start()

    halo_start(1, 0)
    hear_next(pull_copy(0), pull_recv.at[0])
    halo_wait(0, 1)

    def dual1_next(lev):
        field = pull_recv[0, lev] + pulled_halo(0, 1, lev) - spread_ref[rows_of(levels + lev), :]
        dual1[1, lev] = field
        pulled[lev] = pull(1, 1, lev, field)

    each_level(dual1_next)
    send_out(dual1, fore1, 0, 1)
    halo_start(1, 1)

    lax.fori_loop(0, width // 16, circulant, 0)
    mix_hi[...], mix_lo[...] = split(mix_ref[...])
    observe(incr, held, held1)
    spread(held1)
    halo_wait(1, 0)

    def dual2_here(lev):
        out_dual[0, lev] = pulled[lev] + pulled_halo(1, 0, lev) - spread_ref[rows_of(lev), :]

    each_level(dual2_here)
    send_out(out_dual, fore2, 1, 0)
    hear_next(pull_copy(1), pull_recv.at[1])
    halo_wait(1, 1)

    def dual2_next(lev):
        out_dual[1, lev] = pull_recv[1, lev] + pulled_halo(1, 1, lev) - spread_ref[rows_of(levels + lev), :]

    each_level(dual2_next)
    send_out(out_dual, fore2, 1, 1)

    for s in (0, 1):
        far_copy(dual1, fore1, 0, s).wait_recv()
        cover(fore1, mixed1, s)
        send_back(mixed1, back1, 2, s)

    hear_prev(prior_copy(0, incr), prior.at[0])
    halo_wait(2, 0)
    halo_wait(2, 1)

    def moved1(lev):
        part[0, lev] = dep[0, lev] + push(2, 0, lev, prior[0, lev])
        part[1, lev] = dep[1, lev] + push(2, 1, lev, incr[0, lev])

    each_level(moved1)

    for s in (0, 1):
        far_copy(out_dual, fore2, 1, s).wait_recv()
        cover(fore2, mixed2, s)
        send_back(mixed2, back2, 3, s)

    for s in (1, 0):
        far_copy(mixed1, back1, 2, s).wait_recv()

        def incr1_of(lev, s=s):
            field = part[s, lev] - back1[s, lev]
            incr1[s, lev] = field
            edge_rows(3, s, lev, field)

        each_level(incr1_of)
        if s == 1:

            @pl.when(has_next)
            def _():
                prior_copy(1, incr1).start()

        halo_start(3, s)

    observe(incr1, held1, out_held)

    def finish(s, lev, before):
        field = dep[s, lev] + push(3, s, lev, before) - back2[s, lev]
        out_incr[s, lev] = field
        slid_send[s, lev] = traj[s, lev] + field

    def slid_copy(s):
        return remote(slid_send.at[s], out_slid.at[s], slid_ssem.at[s], slid_rsem.at[s], (grp - 1, me))

    for s in (1, 0):
        if s == 0:
            hear_prev(prior_copy(1, incr1), prior.at[1])
        halo_wait(3, s)
        far_copy(mixed2, back2, 3, s).wait_recv()
        each_level(lambda lev, s=s: finish(s, lev, prior[1, lev] if s == 0 else incr1[0, lev]))

        @pl.when(has_prev)
        def _(s=s):
            slid_copy(s).start()

    @pl.when(jnp.logical_not(has_next))
    def _():
        def stay(lev):
            for s in (0, 1):
                out_slid[s, lev] = slid_send[1, lev]

        each_level(stay)

    for s in (0, 1):

        @pl.when(has_next)
        def _(s=s):
            slid_copy(s).wait_recv()

    for s in (0, 1):
        far_copy(dual1, fore1, 0, s).wait_send()
        far_copy(out_dual, fore2, 1, s).wait_send()
        far_copy(mixed1, back1, 2, s).wait_send()
        far_copy(mixed2, back2, 3, s).wait_send()
    for phase in range(4):
        for way in (0, 1):
            for s in (0, 1):

                @pl.when(halo_sends(phase, way, s))
                def _(phase=phase, way=way, s=s):
                    halo(phase, way, s).wait_send()

    @pl.when(has_prev)
    def _():
        pull_copy(0).wait_send()
        pull_copy(1).wait_send()
        slid_copy(0).wait_send()
        slid_copy(1).wait_send()

    @pl.when(has_next)
    def _():
        prior_copy(0, incr).wait_send()
        prior_copy(1, incr1).wait_send()


def circulant_rows(spectrum, width):
    modes, cells = np.arange(width // 2 + 1), np.arange(width)
    weight = np.where((modes == 0) | (modes == width // 2), 1.0, 2.0) / width
    angle = (modes[:, None] * cells[None, :] % width) * (2.0 * math.pi / width)
    table = jnp.asarray((np.cos(angle) * weight[:, None]).astype(np.float32))
    response = jnp.sum(table * spectrum[:, None], axis=0)
    return jnp.stack([jnp.roll(response, i) for i in range(ROWS)])


def on_device(
    departures,
    innovations,
    obs_variance,
    dual_state,
    obs_dual,
    increment,
    trajectory,
    lat_mix,
    spectrum,
    error_scale,
    obs_time,
    obs_level,
    obs_point,
):
    groups, bands = lax.axis_size("tm"), lax.axis_size("space")
    windows, levels, rows, width = increment.shape
    lats = bands * rows
    obs = obs_dual.shape[0]
    cells = windows * levels * rows
    base = circulant_rows(spectrum, width)
    flat = [v.reshape(1, obs) for v in (innovations, obs_variance, obs_dual, obs_time, obs_level, obs_point)]
    state = jax.ShapeDtypeStruct(increment.shape, F32)
    vmem = pl.BlockSpec(memory_space=pltpu.VMEM)
    whole = pltpu.VMEM(increment.shape, F32)
    pencil = pltpu.VMEM((windows, lats, width), F32)
    window = pltpu.VMEM((levels, rows, width), F32)
    window2 = pltpu.VMEM((2, levels, rows, width), F32)
    edge = pltpu.VMEM((4, 2, 2, levels, width), F32)
    dma = pltpu.SemaphoreType.DMA
    dual, held, incr, slid = pl.pallas_call(
        functools.partial(kernel, groups, bands),
        out_shape=(state, jax.ShapeDtypeStruct((1, obs), F32), state, state),
        in_specs=[vmem, vmem, pl.BlockSpec(memory_space=pltpu.SMEM)] + [vmem] * 10,
        out_specs=(vmem,) * 4,
        scratch_shapes=[
            whole,
            whole,
            pltpu.VMEM((width, width), BF16),
            pltpu.VMEM((width, width), BF16),
            pltpu.VMEM((lats, lats), BF16),
            pltpu.VMEM((lats, lats), BF16),
            pltpu.VMEM((1, obs), jnp.int32),
            pltpu.VMEM((1, obs), jnp.int32),
            pltpu.VMEM((cells, obs), BF16),
            pltpu.VMEM((cells, width), F32),
            pltpu.VMEM((width, cells), BF16),
            pltpu.VMEM((width, cells), BF16),
            pltpu.VMEM((1, obs), F32),
            whole,
            window,
            window2,
            window2,
            window2,
            whole,
            whole,
            whole,
            pencil,
            pencil,
            pencil,
            pencil,
            whole,
            whole,
            edge,
            edge,
            dma((4, 2)),
            dma((4, 2)),
            dma((2,)),
            dma((2,)),
            dma((2,)),
            dma((2,)),
            dma((2,)),
            dma((2,)),
            dma((4, 2, 2)),
            dma((4, 2, 2)),
        ],
        compiler_params=pltpu.CompilerParams(
            collective_id=0, has_side_effects=True, vmem_limit_bytes=56 * 1024 * 1024
        ),
    )(
        base,
        lat_mix,
        error_scale,
        departures,
        dual_state,
        increment,
        trajectory,
        *flat,
    )
    return (dual, held.reshape(obs), incr, slid)


def solution(mesh):
    state = P("tm", None, "space", None)
    flat = P(("tm", "space"))
    placed = (state, flat, flat, state, flat, state, state, P(), P(), P("tm"), flat, flat, flat)
    return jax.shard_map(
        on_device,
        mesh=mesh,
        in_specs=placed,
        out_specs=(state, flat, state, state),
        check_vma=False,
    )
```

```python
import functools
import math

import jax
import jax.numpy as jnp
import numpy as np
from jax import lax
from jax.experimental import pallas as pl
from jax.experimental.pallas import tpu as pltpu
from jax.sharding import PartitionSpec as P

MESH = pl.DeviceIdType.MESH
ROWS = 8
GROUP = 4
F32 = jnp.float32
BF16 = jnp.bfloat16
SINE = (-2.5052108385e-8, 2.7557319224e-6, -1.9841269841e-4, 8.3333333333e-3, -1.6666666667e-1)


def sine(angle):
    turns = jnp.floor(angle * (1.0 / math.pi) + 0.5)
    rest = angle - turns * 3.140625
    rest = rest - turns * 9.67653589793e-4
    square = rest * rest
    series = SINE[0]
    for factor in SINE[1:]:
        series = series * square + factor
    half = turns * 0.5
    sign = 1.0 - 4.0 * (half - jnp.floor(half))
    return sign * (rest + rest * square * series)


def split(values):
    high = values.astype(BF16)
    return high, (values - high.astype(F32)).astype(BF16)


def dot(left, right, dims=((1,), (0,))):
    return lax.dot_general(left, right, (dims, ((), ())), preferred_element_type=F32)


def kernel(
    groups,
    bands,
    scale_ref,
    table_any,
    mix_any,
    dep_any,
    dual_any,
    incr_any,
    traj_any,
    spectrum_ref,
    innov,
    variance,
    held,
    time_ref,
    level_ref,
    point_ref,
    dual_any_out,
    out_held,
    incr_any_out,
    slid_any_out,
    table,
    mix_ref,
    dep,
    dual,
    incr,
    traj,
    out_dual,
    out_incr,
    east,
    north,
    zonal_hi,
    zonal_lo,
    mix_hi,
    mix_lo,
    row_ref,
    lon_ref,
    row_table,
    spread_ref,
    turned_hi,
    turned_lo,
    held1,
    dual1,
    pulled,
    pull_send,
    pull_recv,
    prior,
    incr1,
    part,
    slid_send,
    fore1,
    fore2,
    mixed1,
    mixed2,
    back1,
    back2,
    halo_send,
    halo_recv,
    far_send,
    far_recv,
    pull_ssem,
    pull_rsem,
    prior_ssem,
    prior_rsem,
    slid_ssem,
    slid_rsem,
    halo_ssem,
    halo_rsem,
    load_sem,
    store_sem,
):
    windows, levels, _, width = dep.shape
    obs = innov.shape[1]
    cells = windows * levels * ROWS
    chunk = min(512, obs)
    me = lax.axis_index("space")
    grp = lax.axis_index("tm")
    has_prev, has_next = grp > 0, grp < groups - 1
    has_below, has_above = me > 0, me < bands - 1
    line = lax.broadcasted_iota(jnp.int32, (ROWS, width), 0)
    is_first, is_last = line == 0, line == ROWS - 1

    loads = {}
    for place, (name, source, target) in enumerate(
        (
            ("traj", traj_any, traj),
            ("dual", dual_any, dual),
            ("incr", incr_any, incr),
            ("dep", dep_any, dep),
            ("table", table_any, table),
            ("mix", mix_any, mix_ref),
        )
    ):
        loads[name] = pltpu.make_async_copy(source, target, load_sem.at[place])

    def both(*flags):
        return functools.reduce(jnp.logical_and, flags)

    for name in ("traj", "dual", "incr"):
        loads[name].start()

    barrier = pltpu.get_barrier_semaphore()
    around = ((0, None), (-1, has_below), (1, has_above))

    def greet(j, carry):
        pl.semaphore_signal(barrier, inc=1, device_id=(grp, lax.rem(me + j, bands)), device_id_type=MESH)
        return carry

    lax.fori_loop(1, bands, greet, 0)
    for shift, there in ((-1, has_prev), (1, has_next)):
        for step, beside in around:
            flags = [there] if beside is None else [there, beside]

            @pl.when(both(*flags))
            def _(shift=shift, step=step):
                pl.semaphore_signal(barrier, inc=1, device_id=(grp + shift, me + step), device_id_type=MESH)

    def await_barrier():
        beside = 1 + has_below.astype(jnp.int32) + has_above.astype(jnp.int32)
        other = has_prev.astype(jnp.int32) + has_next.astype(jnp.int32)
        pl.semaphore_wait(barrier, bands - 1 + other * beside)

    def remote(source, target, ssem, rsem, device):
        return pltpu.make_async_remote_copy(
            src_ref=source, dst_ref=target, send_sem=ssem, recv_sem=rsem, device_id=device, device_id_type=MESH
        )

    def each_level(body):
        def step(i, carry):
            for u in range(GROUP):
                body(i * GROUP + u)
            return carry

        lax.fori_loop(0, levels // GROUP, step, 0)

    def rows_of(j):
        return pl.ds(pl.multiple_of(j * ROWS, ROWS), ROWS)

    def send_out(source, target, k, s):
        def step(j, carry):
            to = lax.rem(me + j, bands)
            remote(source.at[s, to], target.at[s, rows_of(me)], far_send.at[k, s], far_recv.at[k, s], (grp, to)).start()
            return carry

        lax.fori_loop(1, bands, step, 0)
        target[s, rows_of(me), :] = source[s, me]

    def send_back(source, target, k, s):
        def step(j, carry):
            to = lax.rem(me + j, bands)
            remote(source.at[s, rows_of(to)], target.at[s, me], far_send.at[k, s], far_recv.at[k, s], (grp, to)).start()
            return carry

        lax.fori_loop(1, bands, step, 0)
        target[s, me] = source[s, rows_of(me), :]

    def all_but_one(ref, s):
        return ref.at[s, pl.ds(0, bands - 1)] if ref.ndim == 4 else ref.at[s, pl.ds(0, (bands - 1) * ROWS)]

    def far_copy(source, target, k, s):
        return remote(all_but_one(source, s), all_but_one(target, s), far_send.at[k, s], far_recv.at[k, s], (grp, me))

    def halo(phase, way, s):
        pulls = phase < 2
        to_group = (grp - 1 if pulls else grp) if s == 0 else (grp if pulls else grp + 1)
        to_band = me + 1 if way == 0 else me - 1
        return remote(
            halo_send.at[phase, way, s],
            halo_recv.at[phase, way, 1 - s],
            halo_ssem.at[phase, way, s],
            halo_rsem.at[phase, way, 1 - s],
            (to_group, to_band),
        )

    def halo_sends(phase, way, s):
        beside = has_above if way == 0 else has_below
        if phase < 2 and s == 0:
            return both(beside, has_prev)
        if phase >= 2 and s == 1:
            return both(beside, has_next)
        return beside

    def halo_hears(phase, way, s):
        beside = has_below if way == 0 else has_above
        if phase < 2 and s == 1:
            return both(beside, has_next)
        if phase >= 2 and s == 0:
            return both(beside, has_prev)
        return beside

    def halo_start(phase, s):
        for way in (0, 1):

            @pl.when(halo_sends(phase, way, s))
            def _(way=way):
                halo(phase, way, s).start()

    def halo_wait(phase, s):
        for way in (0, 1):

            @pl.when(halo_hears(phase, way, s))
            def _(way=way):
                halo(phase, way, 1 - s).wait_recv()

            @pl.when(jnp.logical_not(halo_hears(phase, way, s)))
            def _(way=way):
                halo_recv[phase, way, s] = jnp.zeros((levels, width), F32)

    def halo_row(phase, way, s, lev):
        return halo_recv[phase, way, s, pl.ds(lev, 1), :]

    def pull_copy(k):
        return remote(pull_send.at[k], pull_recv.at[k], pull_ssem.at[k], pull_rsem.at[k], (grp - 1, me))

    def prior_copy(k, source):
        return remote(source.at[1], prior.at[k], prior_ssem.at[k], prior_rsem.at[k], (grp + 1, me))

    def hear_next(copy, buffer):
        @pl.when(has_next)
        def _():
            copy.wait_recv()

        @pl.when(jnp.logical_not(has_next))
        def _():
            buffer[...] = jnp.zeros(buffer.shape, F32)

    def hear_prev(copy, buffer):
        @pl.when(has_prev)
        def _():
            copy.wait_recv()

        @pl.when(jnp.logical_not(has_prev))
        def _():
            buffer[...] = jnp.zeros(buffer.shape, F32)

    def pull(phase, s, lev, field):
        pe, pn = east[s, lev], north[s, lev]
        down = field * pn
        up = field * (0.2 - pn)
        halo_send[phase, 0, s, pl.ds(lev, 1), :] = up[ROWS - 1 :, :]
        halo_send[phase, 1, s, pl.ds(lev, 1), :] = down[:1, :]
        return (
            0.6 * field
            + pltpu.roll(field * pe, width - 1, 1)
            + pltpu.roll(field * (0.2 - pe), 1, 1)
            + jnp.where(is_last, 0.0, pltpu.roll(down, ROWS - 1, 0))
            + jnp.where(is_first, 0.0, pltpu.roll(up, 1, 0))
        )

    def pulled_halo(phase, s, lev):
        return jnp.where(is_first, halo_row(phase, 0, s, lev), 0.0) + jnp.where(is_last, halo_row(phase, 1, s, lev), 0.0)

    def push(phase, s, lev, field):
        pe, pn = east[s, lev], north[s, lev]
        above = jnp.where(is_last, halo_row(phase, 1, s, lev), pltpu.roll(field, ROWS - 1, 0))
        below = jnp.where(is_first, halo_row(phase, 0, s, lev), pltpu.roll(field, 1, 0))
        return (
            0.6 * field
            + pltpu.roll(field, width - 1, 1) * (0.2 - pe)
            + pltpu.roll(field, 1, 1) * pe
            + above * (0.2 - pn)
            + below * pn
        )

    def edge_rows(phase, s, lev, field):
        halo_send[phase, 0, s, pl.ds(lev, 1), :] = field[ROWS - 1 :, :]
        halo_send[phase, 1, s, pl.ds(lev, 1), :] = field[:1, :]

    def piece(c):
        return pl.ds(pl.multiple_of(c * chunk, chunk), chunk)

    def tables():
        shift = width.bit_length() - 1
        point = point_ref[...]
        row_ref[...] = ((time_ref[...] - grp * windows) * levels + level_ref[...]) * ROWS + (
            lax.shift_right_logical(point, shift) - me * ROWS
        )
        lon_ref[...] = jnp.bitwise_and(point, width - 1)

        def step(c, carry):
            wanted = row_ref[:, piece(c)]
            block = 64
            for r in range(0, cells, block):
                spot = lax.broadcasted_iota(jnp.int32, (block, chunk), 0) + r
                row_table[r : r + block, piece(c)] = jnp.where(spot == wanted, 1.0, 0.0).astype(BF16)
            return carry

        lax.fori_loop(0, obs // chunk, step, 0)

    def spread(values):
        spread_ref[...] = jnp.zeros(spread_ref.shape, F32)

        def step(c, carry):
            weight = values[:, piece(c)]
            high = weight.astype(BF16).astype(F32)
            low = weight - high
            hit = lax.broadcasted_iota(jnp.int32, (width, chunk), 0) == lon_ref[:, piece(c)]
            chosen = row_table[:, piece(c)]
            total = dot(chosen, jnp.where(hit, high, 0.0).astype(BF16), ((1,), (1,)))
            total = total + dot(chosen, jnp.where(hit, low, 0.0).astype(BF16), ((1,), (1,)))
            spread_ref[...] += total
            return carry

        lax.fori_loop(0, obs // chunk, step, 0)

    def observe(state, old, new):
        turned = state[...].reshape(cells, width).T
        turned_hi[...], turned_lo[...] = split(turned)

        def step(c, carry):
            chosen = row_table[:, piece(c)]
            picked = dot(turned_hi[...], chosen) + dot(turned_lo[...], chosen)
            hit = lax.broadcasted_iota(jnp.int32, (width, chunk), 0) == lon_ref[:, piece(c)]
            seen = jnp.sum(jnp.where(hit, picked, 0.0), axis=0, keepdims=True)
            spread_of, before = variance[:, piece(c)], old[:, piece(c)]
            new[:, piece(c)] = before + (innov[:, piece(c)] - spread_of * before - seen) / spread_of
            return carry

        lax.fori_loop(0, obs // chunk, step, 0)

    def cover(source, target, s):
        high, low = split(source[s])
        smooth = dot(high, zonal_hi[...]) + (dot(high, zonal_lo[...]) + dot(low, zonal_hi[...]))
        high, low = split(smooth)
        mixed = smooth + (dot(mix_hi[...], high) + (dot(mix_hi[...], low) + dot(mix_lo[...], high)))
        target[s] = mixed

    def first(lev):
        for s in (0, 1):
            wind = traj[s, lev]
            east[s, lev] = 0.1 + 0.25 * jnp.tanh(wind)
            north[s, lev] = 0.1 + 0.25 * sine(wind)
            value = pull(0, s, lev, dual[s, lev])
            if s == 0:
                pull_send[0, lev] = value
            else:
                pulled[lev] = value
            edge_rows(2, s, lev, incr[s, lev])

    for name in ("dep", "table", "mix"):
        loads[name].start()
    for name in ("traj", "dual", "incr"):
        loads[name].wait()
    each_level(first)
    await_barrier()

    @pl.when(has_prev)
    def _():
        pull_copy(0).start()

    for s in (1, 0):
        halo_start(0, s)

    @pl.when(has_next)
    def _():
        prior_copy(0, incr).start()

    for s in (0, 1):
        halo_start(2, s)

    tables()
    spread(held)

    def response():
        modes = width // 2
        row = jnp.broadcast_to(spectrum_ref[pl.ds(0, modes)].reshape(1, modes), (ROWS, modes))
        high, low = split(row)
        table_hi, table_lo = split(table[...])
        first = dot(high, table_hi) + (dot(high, table_lo) + dot(low, table_hi))
        cell = lax.broadcasted_iota(jnp.int32, (ROWS, width), 1)
        parity = 1.0 - 2.0 * jnp.bitwise_and(cell, 1).astype(F32)
        first = first + parity * (spectrum_ref[pl.ds(modes, 1)].reshape(1, 1) * (1.0 / width))
        rows = first
        for step in range(1, ROWS):
            rows = jnp.where(line == step, pltpu.roll(first, step, 1), rows)
        return rows

    def circulant(rows, a, carry):
        tall = [pltpu.roll(rows, a * 16 + t, 1) for t in (0, 8)]
        high, low = split(jnp.concatenate(tall, axis=0))
        at = pl.ds(pl.multiple_of(a * 16, 16), 16)
        zonal_hi[at, :] = high
        zonal_lo[at, :] = low
        return carry

    halo_wait(0, 0)

    def dual1_here(lev):
        field = pulled[lev] + pulled_halo(0, 0, lev) - spread_ref[rows_of(lev), :]
        dual1[0, lev] = field
        pull_send[1, lev] = pull(1, 0, lev, field)

    each_level(dual1_here)
    send_out(dual1, fore1, 0, 0)

    @pl.when(has_prev)
    def _():
        pull_copy(1).start()

    halo_start(1, 0)
    hear_next(pull_copy(0), pull_recv.at[0])
    halo_wait(0, 1)

    def dual1_next(lev):
        field = pull_recv[0, lev] + pulled_halo(0, 1, lev) - spread_ref[rows_of(levels + lev), :]
        dual1[1, lev] = field
        pulled[lev] = pull(1, 1, lev, field)

    each_level(dual1_next)
    send_out(dual1, fore1, 0, 1)
    halo_start(1, 1)

    for name in ("dep", "table", "mix"):
        loads[name].wait()
    lax.fori_loop(0, width // 16, functools.partial(circulant, response()), 0)
    mix_hi[...], mix_lo[...] = split(mix_ref[...])
    observe(incr, held, held1)
    spread(held1)
    halo_wait(1, 0)

    def dual2_here(lev):
        out_dual[0, lev] = pulled[lev] + pulled_halo(1, 0, lev) - spread_ref[rows_of(lev), :]

    each_level(dual2_here)
    send_out(out_dual, fore2, 1, 0)
    hear_next(pull_copy(1), pull_recv.at[1])
    halo_wait(1, 1)

    def dual2_next(lev):
        out_dual[1, lev] = pull_recv[1, lev] + pulled_halo(1, 1, lev) - spread_ref[rows_of(levels + lev), :]

    each_level(dual2_next)
    dual_store = pltpu.make_async_copy(out_dual, dual_any_out, store_sem.at[0])
    dual_store.start()
    send_out(out_dual, fore2, 1, 1)

    for s in (0, 1):
        far_copy(dual1, fore1, 0, s).wait_recv()
        cover(fore1, mixed1, s)
        send_back(mixed1, back1, 2, s)

    hear_prev(prior_copy(0, incr), prior.at[0])
    halo_wait(2, 0)
    halo_wait(2, 1)

    def moved1(lev):
        part[0, lev] = dep[0, lev] + push(2, 0, lev, prior[0, lev])
        part[1, lev] = dep[1, lev] + push(2, 1, lev, incr[0, lev])

    each_level(moved1)

    for s in (0, 1):
        far_copy(out_dual, fore2, 1, s).wait_recv()
        cover(fore2, mixed2, s)
        send_back(mixed2, back2, 3, s)

    for s in (1, 0):
        far_copy(mixed1, back1, 2, s).wait_recv()

        def incr1_of(lev, s=s):
            field = part[s, lev] - back1[s, lev] * (scale_ref[s] * scale_ref[s])
            incr1[s, lev] = field
            edge_rows(3, s, lev, field)

        each_level(incr1_of)
        if s == 1:

            @pl.when(has_next)
            def _():
                prior_copy(1, incr1).start()

        halo_start(3, s)

    observe(incr1, held1, out_held)

    def finish(s, lev, before):
        field = dep[s, lev] + push(3, s, lev, before) - back2[s, lev] * (scale_ref[s] * scale_ref[s])
        out_incr[s, lev] = field
        slid_send[s, lev] = traj[s, lev] + field

    def slid_copy(s):
        return remote(slid_send.at[s], slid_any_out.at[s], slid_ssem.at[s], slid_rsem.at[s], (grp - 1, me))

    def incr_store(s):
        return pltpu.make_async_copy(out_incr.at[s], incr_any_out.at[s], store_sem.at[1 + s])

    def stay(s):
        return pltpu.make_async_copy(slid_send.at[1], slid_any_out.at[s], store_sem.at[3 + s])

    for s in (1, 0):
        if s == 0:
            hear_prev(prior_copy(1, incr1), prior.at[1])
        halo_wait(3, s)
        far_copy(mixed2, back2, 3, s).wait_recv()
        each_level(lambda lev, s=s: finish(s, lev, prior[1, lev] if s == 0 else incr1[0, lev]))

        @pl.when(has_prev)
        def _(s=s):
            slid_copy(s).start()

        incr_store(s).start()

    @pl.when(jnp.logical_not(has_next))
    def _():
        for s in (0, 1):
            stay(s).start()
        for s in (0, 1):
            stay(s).wait()

    for s in (0, 1):

        @pl.when(has_next)
        def _(s=s):
            slid_copy(s).wait_recv()

    dual_store.wait()
    for s in (0, 1):
        incr_store(s).wait()
    for s in (0, 1):
        far_copy(dual1, fore1, 0, s).wait_send()
        far_copy(out_dual, fore2, 1, s).wait_send()
        far_copy(mixed1, back1, 2, s).wait_send()
        far_copy(mixed2, back2, 3, s).wait_send()
    for phase in range(4):
        for way in (0, 1):
            for s in (0, 1):

                @pl.when(halo_sends(phase, way, s))
                def _(phase=phase, way=way, s=s):
                    halo(phase, way, s).wait_send()

    @pl.when(has_prev)
    def _():
        pull_copy(0).wait_send()
        pull_copy(1).wait_send()
        slid_copy(0).wait_send()
        slid_copy(1).wait_send()

    @pl.when(has_next)
    def _():
        prior_copy(0, incr).wait_send()
        prior_copy(1, incr1).wait_send()


def cosine_table(width):
    modes, cells = np.arange(width // 2), np.arange(width)
    weight = np.where(modes == 0, 1.0, 2.0) / width
    angle = (modes[:, None] * cells[None, :] % width) * (2.0 * math.pi / width)
    return jnp.asarray((np.cos(angle) * weight[:, None]).astype(np.float32))


def hand_over(count, *refs):
    sources, targets, held = refs[:count], refs[count : 2 * count], refs[2 * count : 3 * count]
    load_sem, store_sem = refs[3 * count :]
    loads = [pltpu.make_async_copy(a, b, load_sem.at[i]) for i, (a, b) in enumerate(zip(sources, held))]
    stores = [pltpu.make_async_copy(a, b, store_sem.at[i]) for i, (a, b) in enumerate(zip(held, targets))]
    for load in loads:
        load.start()
    for load, store in zip(loads, stores):
        load.wait()
        store.start()
    for store in stores:
        store.wait()


def on_device(
    departures,
    innovations,
    obs_variance,
    dual_state,
    obs_dual,
    increment,
    trajectory,
    lat_mix,
    spectrum,
    error_scale,
    obs_time,
    obs_level,
    obs_point,
):
    groups, bands = lax.axis_size("tm"), lax.axis_size("space")
    windows, levels, rows, width = increment.shape
    lats = bands * rows
    obs = obs_dual.shape[0]
    cells = windows * levels * rows
    flat = [v.reshape(1, obs) for v in (innovations, obs_variance, obs_dual, obs_time, obs_level, obs_point)]
    state = jax.ShapeDtypeStruct(increment.shape, F32)
    held_shape = jax.ShapeDtypeStruct((1, obs), F32)
    vmem = pl.BlockSpec(memory_space=pltpu.VMEM)
    anywhere = pl.BlockSpec(memory_space=pl.ANY)
    whole = pltpu.VMEM(increment.shape, F32)
    pencil = pltpu.VMEM((windows, lats, width), F32)
    window = pltpu.VMEM((levels, rows, width), F32)
    window2 = pltpu.VMEM((2, levels, rows, width), F32)
    edge = pltpu.VMEM((4, 2, 2, levels, width), F32)
    dma = pltpu.SemaphoreType.DMA
    dual, held, incr, slid = pl.pallas_call(
        functools.partial(kernel, groups, bands),
        out_shape=(state, held_shape, state, state),
        in_specs=[pl.BlockSpec(memory_space=pltpu.SMEM)] + [anywhere] * 6 + [vmem] * 7,
        out_specs=(anywhere, vmem, anywhere, anywhere),
        scratch_shapes=[
            pltpu.VMEM((width // 2, width), F32),
            pltpu.VMEM((lats, lats), F32),
            whole,
            whole,
            whole,
            whole,
            whole,
            whole,
            whole,
            whole,
            pltpu.VMEM((width, width), BF16),
            pltpu.VMEM((width, width), BF16),
            pltpu.VMEM((lats, lats), BF16),
            pltpu.VMEM((lats, lats), BF16),
            pltpu.VMEM((1, obs), jnp.int32),
            pltpu.VMEM((1, obs), jnp.int32),
            pltpu.VMEM((cells, obs), BF16),
            pltpu.VMEM((cells, width), F32),
            pltpu.VMEM((width, cells), BF16),
            pltpu.VMEM((width, cells), BF16),
            pltpu.VMEM((1, obs), F32),
            whole,
            window,
            window2,
            window2,
            window2,
            whole,
            whole,
            whole,
            pencil,
            pencil,
            pencil,
            pencil,
            whole,
            whole,
            edge,
            edge,
            dma((4, 2)),
            dma((4, 2)),
            dma((2,)),
            dma((2,)),
            dma((2,)),
            dma((2,)),
            dma((2,)),
            dma((2,)),
            dma((4, 2, 2)),
            dma((4, 2, 2)),
            dma((6,)),
            dma((5,)),
        ],
        compiler_params=pltpu.CompilerParams(
            collective_id=0, has_side_effects=True, vmem_limit_bytes=56 * 1024 * 1024
        ),
    )(
        error_scale,
        cosine_table(width),
        lat_mix,
        departures,
        dual_state,
        increment,
        trajectory,
        spectrum,
        *flat,
    )
    memory = pl.BlockSpec(memory_space=pltpu.HBM)
    dual, held, incr, slid = pl.pallas_call(
        functools.partial(hand_over, 4),
        out_shape=(state, held_shape, state, state),
        in_specs=[memory] * 4,
        out_specs=(memory,) * 4,
        scratch_shapes=[whole, pltpu.VMEM((1, obs), F32), whole, whole, dma((4,)), dma((4,))],
    )(dual, held, incr, slid)
    return (dual, held.reshape(obs), incr, slid)


def solution(mesh):
    state = P("tm", None, "space", None)
    flat = P(("tm", "space"))
    placed = (state, flat, flat, state, flat, state, state, P(), P(), P("tm"), flat, flat, flat)
    return jax.shard_map(
        on_device,
        mesh=mesh,
        in_specs=placed,
        out_specs=(state, flat, state, state),
        check_vma=False,
    )
```

```python
import functools
import math

import jax
import jax.numpy as jnp
import numpy as np
from jax import lax
from jax.experimental import pallas as pl
from jax.experimental.pallas import tpu as pltpu
from jax.sharding import PartitionSpec as P

MESH = pl.DeviceIdType.MESH
ROWS = 8
GROUP = 4
F32 = jnp.float32
BF16 = jnp.bfloat16
SINE = (-2.5052108385e-8, 2.7557319224e-6, -1.9841269841e-4, 8.3333333333e-3, -1.6666666667e-1)


def sine(angle):
    turns = jnp.floor(angle * (1.0 / math.pi) + 0.5)
    rest = angle - turns * 3.140625
    rest = rest - turns * 9.67653589793e-4
    square = rest * rest
    series = SINE[0]
    for factor in SINE[1:]:
        series = series * square + factor
    half = turns * 0.5
    sign = 1.0 - 4.0 * (half - jnp.floor(half))
    return sign * (rest + rest * square * series)


def split(values):
    high = values.astype(BF16)
    return high, (values - high.astype(F32)).astype(BF16)


def dot(left, right, dims=((1,), (0,))):
    return lax.dot_general(left, right, (dims, ((), ())), preferred_element_type=F32)


def kernel(
    groups,
    bands,
    scale_ref,
    table_any,
    mix_any,
    dep_any,
    dual_any,
    incr_any,
    traj_any,
    spectrum_ref,
    innov,
    variance,
    held,
    time_ref,
    level_ref,
    point_ref,
    dual_any_out,
    out_held,
    incr_any_out,
    slid_any_out,
    table,
    mix_ref,
    dep,
    dual,
    incr,
    traj,
    out_dual,
    out_incr,
    east,
    north,
    zonal_hi,
    zonal_lo,
    mix_hi,
    mix_lo,
    row_ref,
    lon_ref,
    row_table,
    spread_ref,
    turned_hi,
    turned_lo,
    held1,
    dual1,
    pulled,
    pull_send,
    pull_recv,
    prior,
    incr1,
    part,
    slid_send,
    fore1,
    fore2,
    mixed1,
    mixed2,
    back1,
    back2,
    halo_send,
    halo_recv,
    far_send,
    far_recv,
    pull_ssem,
    pull_rsem,
    prior_ssem,
    prior_rsem,
    slid_ssem,
    slid_rsem,
    halo_ssem,
    halo_rsem,
    load_sem,
    store_sem,
):
    windows, levels, _, width = dep.shape
    obs = innov.shape[1]
    cells = windows * levels * ROWS
    chunk = min(512, obs)
    me = lax.axis_index("space")
    grp = lax.axis_index("tm")
    has_prev, has_next = grp > 0, grp < groups - 1
    has_below, has_above = me > 0, me < bands - 1
    line = lax.broadcasted_iota(jnp.int32, (ROWS, width), 0)
    is_first, is_last = line == 0, line == ROWS - 1

    loads = {}
    for place, (name, source, target) in enumerate(
        (
            ("traj", traj_any, traj),
            ("dual", dual_any, dual),
            ("incr", incr_any, incr),
            ("dep", dep_any, dep),
            ("table", table_any, table),
            ("mix", mix_any, mix_ref),
        )
    ):
        loads[name] = pltpu.make_async_copy(source, target, load_sem.at[place])

    def both(*flags):
        return functools.reduce(jnp.logical_and, flags)

    for name in ("traj", "dual", "incr"):
        loads[name].start()

    barrier = pltpu.get_barrier_semaphore()
    around = ((0, None), (-1, has_below), (1, has_above))

    def greet(j, carry):
        pl.semaphore_signal(barrier, inc=1, device_id=(grp, lax.rem(me + j, bands)), device_id_type=MESH)
        return carry

    lax.fori_loop(1, bands, greet, 0)
    for shift, there in ((-1, has_prev), (1, has_next)):
        for step, beside in around:
            flags = [there] if beside is None else [there, beside]

            @pl.when(both(*flags))
            def _(shift=shift, step=step):
                pl.semaphore_signal(barrier, inc=1, device_id=(grp + shift, me + step), device_id_type=MESH)

    def await_barrier():
        beside = 1 + has_below.astype(jnp.int32) + has_above.astype(jnp.int32)
        other = has_prev.astype(jnp.int32) + has_next.astype(jnp.int32)
        pl.semaphore_wait(barrier, bands - 1 + other * beside)

    def remote(source, target, ssem, rsem, device):
        return pltpu.make_async_remote_copy(
            src_ref=source, dst_ref=target, send_sem=ssem, recv_sem=rsem, device_id=device, device_id_type=MESH
        )

    def each_level(body):
        def step(i, carry):
            for u in range(GROUP):
                body(i * GROUP + u)
            return carry

        lax.fori_loop(0, levels // GROUP, step, 0)

    def rows_of(j):
        return pl.ds(pl.multiple_of(j * ROWS, ROWS), ROWS)

    def send_out(source, target, k, s):
        def step(j, carry):
            to = lax.rem(me + j, bands)
            remote(source.at[s, to], target.at[s, rows_of(me)], far_send.at[k, s], far_recv.at[k, s], (grp, to)).start()
            return carry

        lax.fori_loop(1, bands, step, 0)
        target[s, rows_of(me), :] = source[s, me]

    def send_back(source, target, k, s):
        def step(j, carry):
            to = lax.rem(me + j, bands)
            remote(source.at[s, rows_of(to)], target.at[s, me], far_send.at[k, s], far_recv.at[k, s], (grp, to)).start()
            return carry

        lax.fori_loop(1, bands, step, 0)
        target[s, me] = source[s, rows_of(me), :]

    def all_but_one(ref, s):
        return ref.at[s, pl.ds(0, bands - 1)] if ref.ndim == 4 else ref.at[s, pl.ds(0, (bands - 1) * ROWS)]

    def far_copy(source, target, k, s):
        return remote(all_but_one(source, s), all_but_one(target, s), far_send.at[k, s], far_recv.at[k, s], (grp, me))

    def halo(phase, way, s):
        pulls = phase < 2
        to_group = (grp - 1 if pulls else grp) if s == 0 else (grp if pulls else grp + 1)
        to_band = me + 1 if way == 0 else me - 1
        return remote(
            halo_send.at[phase, way, s],
            halo_recv.at[phase, way, 1 - s],
            halo_ssem.at[phase, way, s],
            halo_rsem.at[phase, way, 1 - s],
            (to_group, to_band),
        )

    def halo_sends(phase, way, s):
        beside = has_above if way == 0 else has_below
        if phase < 2 and s == 0:
            return both(beside, has_prev)
        if phase >= 2 and s == 1:
            return both(beside, has_next)
        return beside

    def halo_hears(phase, way, s):
        beside = has_below if way == 0 else has_above
        if phase < 2 and s == 1:
            return both(beside, has_next)
        if phase >= 2 and s == 0:
            return both(beside, has_prev)
        return beside

    def halo_start(phase, s):
        for way in (0, 1):

            @pl.when(halo_sends(phase, way, s))
            def _(way=way):
                halo(phase, way, s).start()

    def halo_wait(phase, s):
        for way in (0, 1):

            @pl.when(halo_hears(phase, way, s))
            def _(way=way):
                halo(phase, way, 1 - s).wait_recv()

            @pl.when(jnp.logical_not(halo_hears(phase, way, s)))
            def _(way=way):
                halo_recv[phase, way, s] = jnp.zeros((levels, width), F32)

    def halo_row(phase, way, s, lev):
        return halo_recv[phase, way, s, pl.ds(lev, 1), :]

    def pull_copy(k):
        return remote(pull_send.at[k], pull_recv.at[k], pull_ssem.at[k], pull_rsem.at[k], (grp - 1, me))

    def prior_copy(k, source):
        return remote(source.at[1], prior.at[k], prior_ssem.at[k], prior_rsem.at[k], (grp + 1, me))

    def hear_next(copy, buffer):
        @pl.when(has_next)
        def _():
            copy.wait_recv()

        @pl.when(jnp.logical_not(has_next))
        def _():
            buffer[...] = jnp.zeros(buffer.shape, F32)

    def hear_prev(copy, buffer):
        @pl.when(has_prev)
        def _():
            copy.wait_recv()

        @pl.when(jnp.logical_not(has_prev))
        def _():
            buffer[...] = jnp.zeros(buffer.shape, F32)

    def pull(phase, s, lev, field):
        pe, pn = east[s, lev], north[s, lev]
        down = field * pn
        up = field * (0.2 - pn)
        halo_send[phase, 0, s, pl.ds(lev, 1), :] = up[ROWS - 1 :, :]
        halo_send[phase, 1, s, pl.ds(lev, 1), :] = down[:1, :]
        return (
            0.6 * field
            + pltpu.roll(field * pe, width - 1, 1)
            + pltpu.roll(field * (0.2 - pe), 1, 1)
            + jnp.where(is_last, 0.0, pltpu.roll(down, ROWS - 1, 0))
            + jnp.where(is_first, 0.0, pltpu.roll(up, 1, 0))
        )

    def pulled_halo(phase, s, lev):
        return jnp.where(is_first, halo_row(phase, 0, s, lev), 0.0) + jnp.where(is_last, halo_row(phase, 1, s, lev), 0.0)

    def push(phase, s, lev, field):
        pe, pn = east[s, lev], north[s, lev]
        above = jnp.where(is_last, halo_row(phase, 1, s, lev), pltpu.roll(field, ROWS - 1, 0))
        below = jnp.where(is_first, halo_row(phase, 0, s, lev), pltpu.roll(field, 1, 0))
        return (
            0.6 * field
            + pltpu.roll(field, width - 1, 1) * (0.2 - pe)
            + pltpu.roll(field, 1, 1) * pe
            + above * (0.2 - pn)
            + below * pn
        )

    def edge_rows(phase, s, lev, field):
        halo_send[phase, 0, s, pl.ds(lev, 1), :] = field[ROWS - 1 :, :]
        halo_send[phase, 1, s, pl.ds(lev, 1), :] = field[:1, :]

    def piece(c):
        return pl.ds(pl.multiple_of(c * chunk, chunk), chunk)

    def tables():
        shift = width.bit_length() - 1
        point = point_ref[...]
        row_ref[...] = ((time_ref[...] - grp * windows) * levels + level_ref[...]) * ROWS + (
            lax.shift_right_logical(point, shift) - me * ROWS
        )
        lon_ref[...] = jnp.bitwise_and(point, width - 1)

        def step(c, carry):
            wanted = row_ref[:, piece(c)]
            block = 64
            for r in range(0, cells, block):
                spot = lax.broadcasted_iota(jnp.int32, (block, chunk), 0) + r
                row_table[r : r + block, piece(c)] = jnp.where(spot == wanted, 1.0, 0.0).astype(BF16)
            return carry

        lax.fori_loop(0, obs // chunk, step, 0)

    def spread(values):
        spread_ref[...] = jnp.zeros(spread_ref.shape, F32)

        def step(c, carry):
            weight = values[:, piece(c)]
            high = weight.astype(BF16).astype(F32)
            low = weight - high
            hit = lax.broadcasted_iota(jnp.int32, (width, chunk), 0) == lon_ref[:, piece(c)]
            chosen = row_table[:, piece(c)]
            total = dot(chosen, jnp.where(hit, high, 0.0).astype(BF16), ((1,), (1,)))
            total = total + dot(chosen, jnp.where(hit, low, 0.0).astype(BF16), ((1,), (1,)))
            spread_ref[...] += total
            return carry

        lax.fori_loop(0, obs // chunk, step, 0)

    def observe(state, old, new):
        turned = state[...].reshape(cells, width).T
        turned_hi[...], turned_lo[...] = split(turned)

        def step(c, carry):
            chosen = row_table[:, piece(c)]
            picked = dot(turned_hi[...], chosen) + dot(turned_lo[...], chosen)
            hit = lax.broadcasted_iota(jnp.int32, (width, chunk), 0) == lon_ref[:, piece(c)]
            seen = jnp.sum(jnp.where(hit, picked, 0.0), axis=0, keepdims=True)
            spread_of, before = variance[:, piece(c)], old[:, piece(c)]
            new[:, piece(c)] = before + (innov[:, piece(c)] - spread_of * before - seen) / spread_of
            return carry

        lax.fori_loop(0, obs // chunk, step, 0)

    def cover(source, target, s):
        high, low = split(source[s])
        smooth = dot(high, zonal_hi[...]) + (dot(high, zonal_lo[...]) + dot(low, zonal_hi[...]))
        high, low = split(smooth)
        mixed = smooth + (dot(mix_hi[...], high) + (dot(mix_hi[...], low) + dot(mix_lo[...], high)))
        target[s] = mixed

    def first(lev):
        for s in (0, 1):
            wind = traj[s, lev]
            east[s, lev] = 0.1 + 0.25 * jnp.tanh(wind)
            north[s, lev] = 0.1 + 0.25 * sine(wind)
            value = pull(0, s, lev, dual[s, lev])
            if s == 0:
                pull_send[0, lev] = value
            else:
                pulled[lev] = value
            edge_rows(2, s, lev, incr[s, lev])

    for name in ("dep", "table", "mix"):
        loads[name].start()
    for name in ("traj", "dual", "incr"):
        loads[name].wait()
    each_level(first)
    await_barrier()

    @pl.when(has_prev)
    def _():
        pull_copy(0).start()

    for s in (1, 0):
        halo_start(0, s)

    @pl.when(has_next)
    def _():
        prior_copy(0, incr).start()

    for s in (0, 1):
        halo_start(2, s)

    tables()
    spread(held)

    def response():
        modes = width // 2
        row = jnp.broadcast_to(spectrum_ref[pl.ds(0, modes)].reshape(1, modes), (ROWS, modes))
        high, low = split(row)
        table_hi, table_lo = split(table[...])
        first = dot(high, table_hi) + (dot(high, table_lo) + dot(low, table_hi))
        cell = lax.broadcasted_iota(jnp.int32, (ROWS, width), 1)
        parity = 1.0 - 2.0 * jnp.bitwise_and(cell, 1).astype(F32)
        first = first + parity * (spectrum_ref[pl.ds(modes, 1)].reshape(1, 1) * (1.0 / width))
        rows = first
        for step in range(1, ROWS):
            rows = jnp.where(line == step, pltpu.roll(first, step, 1), rows)
        return rows

    def circulant(rows, a, carry):
        tall = [pltpu.roll(rows, a * 16 + t, 1) for t in (0, 8)]
        high, low = split(jnp.concatenate(tall, axis=0))
        at = pl.ds(pl.multiple_of(a * 16, 16), 16)
        zonal_hi[at, :] = high
        zonal_lo[at, :] = low
        return carry

    halo_wait(0, 0)

    def dual1_here(lev):
        field = pulled[lev] + pulled_halo(0, 0, lev) - spread_ref[rows_of(lev), :]
        dual1[0, lev] = field
        pull_send[1, lev] = pull(1, 0, lev, field)

    each_level(dual1_here)

    @pl.when(has_prev)
    def _():
        pull_copy(1).start()

    halo_start(1, 0)
    send_out(dual1, fore1, 0, 0)
    hear_next(pull_copy(0), pull_recv.at[0])
    halo_wait(0, 1)

    def dual1_next(lev):
        field = pull_recv[0, lev] + pulled_halo(0, 1, lev) - spread_ref[rows_of(levels + lev), :]
        dual1[1, lev] = field
        pulled[lev] = pull(1, 1, lev, field)

    each_level(dual1_next)
    halo_start(1, 1)
    send_out(dual1, fore1, 0, 1)

    for name in ("dep", "table", "mix"):
        loads[name].wait()
    lax.fori_loop(0, width // 16, functools.partial(circulant, response()), 0)
    mix_hi[...], mix_lo[...] = split(mix_ref[...])
    observe(incr, held, held1)
    spread(held1)
    halo_wait(1, 0)

    def dual2_here(lev):
        out_dual[0, lev] = pulled[lev] + pulled_halo(1, 0, lev) - spread_ref[rows_of(lev), :]

    each_level(dual2_here)
    send_out(out_dual, fore2, 1, 0)
    hear_next(pull_copy(1), pull_recv.at[1])
    halo_wait(1, 1)

    def dual2_next(lev):
        out_dual[1, lev] = pull_recv[1, lev] + pulled_halo(1, 1, lev) - spread_ref[rows_of(levels + lev), :]

    each_level(dual2_next)
    dual_store = pltpu.make_async_copy(out_dual, dual_any_out, store_sem.at[0])
    dual_store.start()
    send_out(out_dual, fore2, 1, 1)

    for s in (0, 1):
        far_copy(dual1, fore1, 0, s).wait_recv()
        cover(fore1, mixed1, s)
        send_back(mixed1, back1, 2, s)

    hear_prev(prior_copy(0, incr), prior.at[0])
    halo_wait(2, 0)
    halo_wait(2, 1)

    def moved1(lev):
        part[0, lev] = dep[0, lev] + push(2, 0, lev, prior[0, lev])
        part[1, lev] = dep[1, lev] + push(2, 1, lev, incr[0, lev])

    each_level(moved1)

    def second_filter():
        for s in (0, 1):
            far_copy(out_dual, fore2, 1, s).wait_recv()
            cover(fore2, mixed2, s)
            send_back(mixed2, back2, 3, s)

    pl.when(grp == groups // 2)(second_filter)

    for s in (1, 0):
        far_copy(mixed1, back1, 2, s).wait_recv()

        def incr1_of(lev, s=s):
            field = part[s, lev] - back1[s, lev] * (scale_ref[s] * scale_ref[s])
            incr1[s, lev] = field
            edge_rows(3, s, lev, field)

        each_level(incr1_of)
        if s == 1:

            @pl.when(has_next)
            def _():
                prior_copy(1, incr1).start()

        halo_start(3, s)

    pl.when(grp != groups // 2)(second_filter)
    observe(incr1, held1, out_held)

    def finish(s, lev, before):
        field = dep[s, lev] + push(3, s, lev, before) - back2[s, lev] * (scale_ref[s] * scale_ref[s])
        out_incr[s, lev] = field
        slid_send[s, lev] = traj[s, lev] + field

    def slid_copy(s):
        return remote(slid_send.at[s], slid_any_out.at[s], slid_ssem.at[s], slid_rsem.at[s], (grp - 1, me))

    def incr_store(s):
        return pltpu.make_async_copy(out_incr.at[s], incr_any_out.at[s], store_sem.at[1 + s])

    def stay(s):
        return pltpu.make_async_copy(slid_send.at[1], slid_any_out.at[s], store_sem.at[3 + s])

    for s in (1, 0):
        if s == 0:
            hear_prev(prior_copy(1, incr1), prior.at[1])
        halo_wait(3, s)
        far_copy(mixed2, back2, 3, s).wait_recv()
        each_level(lambda lev, s=s: finish(s, lev, prior[1, lev] if s == 0 else incr1[0, lev]))

        @pl.when(has_prev)
        def _(s=s):
            slid_copy(s).start()

        incr_store(s).start()

    @pl.when(jnp.logical_not(has_next))
    def _():
        for s in (0, 1):
            stay(s).start()
        for s in (0, 1):
            stay(s).wait()

    for s in (0, 1):

        @pl.when(has_next)
        def _(s=s):
            slid_copy(s).wait_recv()

    dual_store.wait()
    for s in (0, 1):
        incr_store(s).wait()
    for s in (0, 1):
        far_copy(dual1, fore1, 0, s).wait_send()
        far_copy(out_dual, fore2, 1, s).wait_send()
        far_copy(mixed1, back1, 2, s).wait_send()
        far_copy(mixed2, back2, 3, s).wait_send()
    for phase in range(4):
        for way in (0, 1):
            for s in (0, 1):

                @pl.when(halo_sends(phase, way, s))
                def _(phase=phase, way=way, s=s):
                    halo(phase, way, s).wait_send()

    @pl.when(has_prev)
    def _():
        pull_copy(0).wait_send()
        pull_copy(1).wait_send()
        slid_copy(0).wait_send()
        slid_copy(1).wait_send()

    @pl.when(has_next)
    def _():
        prior_copy(0, incr).wait_send()
        prior_copy(1, incr1).wait_send()


def cosine_table(width):
    modes, cells = np.arange(width // 2), np.arange(width)
    weight = np.where(modes == 0, 1.0, 2.0) / width
    angle = (modes[:, None] * cells[None, :] % width) * (2.0 * math.pi / width)
    return jnp.asarray((np.cos(angle) * weight[:, None]).astype(np.float32))


def hand_over(count, *refs):
    sources, targets, held = refs[:count], refs[count : 2 * count], refs[2 * count : 3 * count]
    load_sem, store_sem = refs[3 * count :]
    loads = [pltpu.make_async_copy(a, b, load_sem.at[i]) for i, (a, b) in enumerate(zip(sources, held))]
    stores = [pltpu.make_async_copy(a, b, store_sem.at[i]) for i, (a, b) in enumerate(zip(held, targets))]
    for load in loads:
        load.start()
    for load, store in zip(loads, stores):
        load.wait()
        store.start()
    for store in stores:
        store.wait()


def on_device(
    departures,
    innovations,
    obs_variance,
    dual_state,
    obs_dual,
    increment,
    trajectory,
    lat_mix,
    spectrum,
    error_scale,
    obs_time,
    obs_level,
    obs_point,
):
    groups, bands = lax.axis_size("tm"), lax.axis_size("space")
    windows, levels, rows, width = increment.shape
    lats = bands * rows
    obs = obs_dual.shape[0]
    cells = windows * levels * rows
    flat = [v.reshape(1, obs) for v in (innovations, obs_variance, obs_dual, obs_time, obs_level, obs_point)]
    state = jax.ShapeDtypeStruct(increment.shape, F32)
    held_shape = jax.ShapeDtypeStruct((1, obs), F32)
    vmem = pl.BlockSpec(memory_space=pltpu.VMEM)
    anywhere = pl.BlockSpec(memory_space=pl.ANY)
    whole = pltpu.VMEM(increment.shape, F32)
    pencil = pltpu.VMEM((windows, lats, width), F32)
    window = pltpu.VMEM((levels, rows, width), F32)
    window2 = pltpu.VMEM((2, levels, rows, width), F32)
    edge = pltpu.VMEM((4, 2, 2, levels, width), F32)
    dma = pltpu.SemaphoreType.DMA
    dual, held, incr, slid = pl.pallas_call(
        functools.partial(kernel, groups, bands),
        out_shape=(state, held_shape, state, state),
        in_specs=[pl.BlockSpec(memory_space=pltpu.SMEM)] + [anywhere] * 6 + [vmem] * 7,
        out_specs=(anywhere, vmem, anywhere, anywhere),
        scratch_shapes=[
            pltpu.VMEM((width // 2, width), F32),
            pltpu.VMEM((lats, lats), F32),
            whole,
            whole,
            whole,
            whole,
            whole,
            whole,
            whole,
            whole,
            pltpu.VMEM((width, width), BF16),
            pltpu.VMEM((width, width), BF16),
            pltpu.VMEM((lats, lats), BF16),
            pltpu.VMEM((lats, lats), BF16),
            pltpu.VMEM((1, obs), jnp.int32),
            pltpu.VMEM((1, obs), jnp.int32),
            pltpu.VMEM((cells, obs), BF16),
            pltpu.VMEM((cells, width), F32),
            pltpu.VMEM((width, cells), BF16),
            pltpu.VMEM((width, cells), BF16),
            pltpu.VMEM((1, obs), F32),
            whole,
            window,
            window2,
            window2,
            window2,
            whole,
            whole,
            whole,
            pencil,
            pencil,
            pencil,
            pencil,
            whole,
            whole,
            edge,
            edge,
            dma((4, 2)),
            dma((4, 2)),
            dma((2,)),
            dma((2,)),
            dma((2,)),
            dma((2,)),
            dma((2,)),
            dma((2,)),
            dma((4, 2, 2)),
            dma((4, 2, 2)),
            dma((6,)),
            dma((5,)),
        ],
        compiler_params=pltpu.CompilerParams(
            collective_id=0, has_side_effects=True, vmem_limit_bytes=56 * 1024 * 1024
        ),
    )(
        error_scale,
        cosine_table(width),
        lat_mix,
        departures,
        dual_state,
        increment,
        trajectory,
        spectrum,
        *flat,
    )
    memory = pl.BlockSpec(memory_space=pltpu.HBM)
    dual, held, incr, slid = pl.pallas_call(
        functools.partial(hand_over, 4),
        out_shape=(state, held_shape, state, state),
        in_specs=[memory] * 4,
        out_specs=(memory,) * 4,
        scratch_shapes=[whole, pltpu.VMEM((1, obs), F32), whole, whole, dma((4,)), dma((4,))],
    )(dual, held, incr, slid)
    return (dual, held.reshape(obs), incr, slid)


def solution(mesh):
    state = P("tm", None, "space", None)
    flat = P(("tm", "space"))
    placed = (state, flat, flat, state, flat, state, state, P(), P(), P("tm"), flat, flat, flat)
    return jax.shard_map(
        on_device,
        mesh=mesh,
        in_specs=placed,
        out_specs=(state, flat, state, state),
        check_vma=False,
    )
```

```python
import functools
import math

import jax
import jax.numpy as jnp
import numpy as np
from jax import lax
from jax.experimental import pallas as pl
from jax.experimental.pallas import tpu as pltpu
from jax.sharding import PartitionSpec as P

MESH = pl.DeviceIdType.MESH
ROWS = 8
GROUP = 4
F32 = jnp.float32
BF16 = jnp.bfloat16
SINE = (-2.5052108385e-8, 2.7557319224e-6, -1.9841269841e-4, 8.3333333333e-3, -1.6666666667e-1)


def sine(angle):
    turns = jnp.floor(angle * (1.0 / math.pi) + 0.5)
    rest = angle - turns * 3.140625
    rest = rest - turns * 9.67653589793e-4
    square = rest * rest
    series = SINE[0]
    for factor in SINE[1:]:
        series = series * square + factor
    half = turns * 0.5
    sign = 1.0 - 4.0 * (half - jnp.floor(half))
    return sign * (rest + rest * square * series)


def split(values):
    high = values.astype(BF16)
    return high, (values - high.astype(F32)).astype(BF16)


def dot(left, right, dims=((1,), (0,))):
    return lax.dot_general(left, right, (dims, ((), ())), preferred_element_type=F32)


def kernel(
    groups,
    bands,
    scale_ref,
    table_any,
    mix_any,
    dep_any,
    dual_any,
    incr_any,
    traj_any,
    spectrum_ref,
    innov,
    variance,
    held,
    time_ref,
    level_ref,
    point_ref,
    dual_any_out,
    out_held,
    incr_any_out,
    slid_any_out,
    table,
    mix_ref,
    dep,
    dual,
    incr,
    traj,
    out_dual,
    out_incr,
    east,
    north,
    zonal_hi,
    zonal_lo,
    mix_hi,
    mix_lo,
    row_ref,
    lon_ref,
    row_table,
    spread_ref,
    turned_hi,
    turned_lo,
    held1,
    dual1,
    pulled,
    pull_send,
    pull_recv,
    prior,
    incr1,
    part,
    slid_send,
    fore1,
    fore2,
    mixed1,
    mixed2,
    back1,
    back2,
    halo_send,
    halo_recv,
    far_send,
    far_recv,
    pull_ssem,
    pull_rsem,
    prior_ssem,
    prior_rsem,
    slid_ssem,
    slid_rsem,
    halo_ssem,
    halo_rsem,
    load_sem,
    store_sem,
):
    windows, levels, _, width = dep.shape
    obs = innov.shape[1]
    cells = windows * levels * ROWS
    chunk = min(2048, obs)
    me = lax.axis_index("space")
    grp = lax.axis_index("tm")
    has_prev, has_next = grp > 0, grp < groups - 1
    has_below, has_above = me > 0, me < bands - 1
    line = lax.broadcasted_iota(jnp.int32, (ROWS, width), 0)
    is_first, is_last = line == 0, line == ROWS - 1

    loads = {}
    for place, (name, source, target) in enumerate(
        (
            ("traj", traj_any, traj),
            ("dual", dual_any, dual),
            ("incr", incr_any, incr),
            ("dep", dep_any, dep),
            ("table", table_any, table),
            ("mix", mix_any, mix_ref),
        )
    ):
        loads[name] = pltpu.make_async_copy(source, target, load_sem.at[place])

    def both(*flags):
        return functools.reduce(jnp.logical_and, flags)

    for name in ("traj", "dual", "incr"):
        loads[name].start()

    barrier = pltpu.get_barrier_semaphore()
    around = ((0, None), (-1, has_below), (1, has_above))

    def greet(j, carry):
        pl.semaphore_signal(barrier, inc=1, device_id=(grp, lax.rem(me + j, bands)), device_id_type=MESH)
        return carry

    lax.fori_loop(1, bands, greet, 0)
    for shift, there in ((-1, has_prev), (1, has_next)):
        for step, beside in around:
            flags = [there] if beside is None else [there, beside]

            @pl.when(both(*flags))
            def _(shift=shift, step=step):
                pl.semaphore_signal(barrier, inc=1, device_id=(grp + shift, me + step), device_id_type=MESH)

    def await_barrier():
        beside = 1 + has_below.astype(jnp.int32) + has_above.astype(jnp.int32)
        other = has_prev.astype(jnp.int32) + has_next.astype(jnp.int32)
        pl.semaphore_wait(barrier, bands - 1 + other * beside)

    def remote(source, target, ssem, rsem, device):
        return pltpu.make_async_remote_copy(
            src_ref=source, dst_ref=target, send_sem=ssem, recv_sem=rsem, device_id=device, device_id_type=MESH
        )

    def each_level(body):
        def step(i, carry):
            for u in range(GROUP):
                body(i * GROUP + u)
            return carry

        lax.fori_loop(0, levels // GROUP, step, 0)

    def rows_of(j):
        return pl.ds(pl.multiple_of(j * ROWS, ROWS), ROWS)

    def send_out(source, target, k, s):
        def step(j, carry):
            to = lax.rem(me + j, bands)
            remote(source.at[s, to], target.at[s, rows_of(me)], far_send.at[k, s], far_recv.at[k, s], (grp, to)).start()
            return carry

        lax.fori_loop(1, bands, step, 0)
        target[s, rows_of(me), :] = source[s, me]

    def send_back(source, target, k, s):
        def step(j, carry):
            to = lax.rem(me + j, bands)
            remote(source.at[s, rows_of(to)], target.at[s, me], far_send.at[k, s], far_recv.at[k, s], (grp, to)).start()
            return carry

        lax.fori_loop(1, bands, step, 0)
        target[s, me] = source[s, rows_of(me), :]

    def all_but_one(ref, s):
        return ref.at[s, pl.ds(0, bands - 1)] if ref.ndim == 4 else ref.at[s, pl.ds(0, (bands - 1) * ROWS)]

    def far_copy(source, target, k, s):
        return remote(all_but_one(source, s), all_but_one(target, s), far_send.at[k, s], far_recv.at[k, s], (grp, me))

    def halo(phase, way, s):
        pulls = phase < 2
        to_group = (grp - 1 if pulls else grp) if s == 0 else (grp if pulls else grp + 1)
        to_band = me + 1 if way == 0 else me - 1
        return remote(
            halo_send.at[phase, way, s],
            halo_recv.at[phase, way, 1 - s],
            halo_ssem.at[phase, way, s],
            halo_rsem.at[phase, way, 1 - s],
            (to_group, to_band),
        )

    def halo_sends(phase, way, s):
        beside = has_above if way == 0 else has_below
        if phase < 2 and s == 0:
            return both(beside, has_prev)
        if phase >= 2 and s == 1:
            return both(beside, has_next)
        return beside

    def halo_hears(phase, way, s):
        beside = has_below if way == 0 else has_above
        if phase < 2 and s == 1:
            return both(beside, has_next)
        if phase >= 2 and s == 0:
            return both(beside, has_prev)
        return beside

    def halo_start(phase, s):
        for way in (0, 1):

            @pl.when(halo_sends(phase, way, s))
            def _(way=way):
                halo(phase, way, s).start()

    def halo_wait(phase, s):
        for way in (0, 1):

            @pl.when(halo_hears(phase, way, s))
            def _(way=way):
                halo(phase, way, 1 - s).wait_recv()

            @pl.when(jnp.logical_not(halo_hears(phase, way, s)))
            def _(way=way):
                halo_recv[phase, way, s] = jnp.zeros((levels, width), F32)

    def halo_row(phase, way, s, lev):
        return halo_recv[phase, way, s, pl.ds(lev, 1), :]

    def pull_copy(k):
        return remote(pull_send.at[k], pull_recv.at[k], pull_ssem.at[k], pull_rsem.at[k], (grp - 1, me))

    def prior_copy(k, source):
        return remote(source.at[1], prior.at[k], prior_ssem.at[k], prior_rsem.at[k], (grp + 1, me))

    def hear_next(copy, buffer):
        @pl.when(has_next)
        def _():
            copy.wait_recv()

        @pl.when(jnp.logical_not(has_next))
        def _():
            buffer[...] = jnp.zeros(buffer.shape, F32)

    def hear_prev(copy, buffer):
        @pl.when(has_prev)
        def _():
            copy.wait_recv()

        @pl.when(jnp.logical_not(has_prev))
        def _():
            buffer[...] = jnp.zeros(buffer.shape, F32)

    def pull(phase, s, lev, field):
        pe, pn = east[s, lev], north[s, lev]
        down = field * pn
        up = field * (0.2 - pn)
        halo_send[phase, 0, s, pl.ds(lev, 1), :] = up[ROWS - 1 :, :]
        halo_send[phase, 1, s, pl.ds(lev, 1), :] = down[:1, :]
        return (
            0.6 * field
            + pltpu.roll(field * pe, width - 1, 1)
            + pltpu.roll(field * (0.2 - pe), 1, 1)
            + jnp.where(is_last, 0.0, pltpu.roll(down, ROWS - 1, 0))
            + jnp.where(is_first, 0.0, pltpu.roll(up, 1, 0))
        )

    def pulled_halo(phase, s, lev):
        return jnp.where(is_first, halo_row(phase, 0, s, lev), 0.0) + jnp.where(is_last, halo_row(phase, 1, s, lev), 0.0)

    def push(phase, s, lev, field):
        pe, pn = east[s, lev], north[s, lev]
        above = jnp.where(is_last, halo_row(phase, 1, s, lev), pltpu.roll(field, ROWS - 1, 0))
        below = jnp.where(is_first, halo_row(phase, 0, s, lev), pltpu.roll(field, 1, 0))
        return (
            0.6 * field
            + pltpu.roll(field, width - 1, 1) * (0.2 - pe)
            + pltpu.roll(field, 1, 1) * pe
            + above * (0.2 - pn)
            + below * pn
        )

    def edge_rows(phase, s, lev, field):
        halo_send[phase, 0, s, pl.ds(lev, 1), :] = field[ROWS - 1 :, :]
        halo_send[phase, 1, s, pl.ds(lev, 1), :] = field[:1, :]

    def piece(c):
        return pl.ds(pl.multiple_of(c * chunk, chunk), chunk)

    def tables():
        shift = width.bit_length() - 1
        point = point_ref[...]
        row_ref[...] = ((time_ref[...] - grp * windows) * levels + level_ref[...]) * ROWS + (
            lax.shift_right_logical(point, shift) - me * ROWS
        )
        lon_ref[...] = jnp.bitwise_and(point, width - 1)

        def step(c, carry):
            wanted = row_ref[:, piece(c)]
            block = 64
            for r in range(0, cells, block):
                spot = lax.broadcasted_iota(jnp.int32, (block, chunk), 0) + r
                row_table[r : r + block, piece(c)] = jnp.where(spot == wanted, 1.0, 0.0).astype(BF16)
            return carry

        lax.fori_loop(0, obs // chunk, step, 0)

    def spread(values):
        spread_ref[...] = jnp.zeros(spread_ref.shape, F32)

        def step(c, carry):
            weight = values[:, piece(c)]
            high = weight.astype(BF16).astype(F32)
            low = weight - high
            hit = lax.broadcasted_iota(jnp.int32, (width, chunk), 0) == lon_ref[:, piece(c)]
            chosen = row_table[:, piece(c)]
            total = dot(chosen, jnp.where(hit, high, 0.0).astype(BF16), ((1,), (1,)))
            total = total + dot(chosen, jnp.where(hit, low, 0.0).astype(BF16), ((1,), (1,)))
            spread_ref[...] += total
            return carry

        lax.fori_loop(0, obs // chunk, step, 0)

    def observe(state, old, new):
        turned = state[...].reshape(cells, width).T
        turned_hi[...], turned_lo[...] = split(turned)

        def step(c, carry):
            chosen = row_table[:, piece(c)]
            picked = dot(turned_hi[...], chosen) + dot(turned_lo[...], chosen)
            hit = lax.broadcasted_iota(jnp.int32, (width, chunk), 0) == lon_ref[:, piece(c)]
            seen = jnp.sum(jnp.where(hit, picked, 0.0), axis=0, keepdims=True)
            spread_of, before = variance[:, piece(c)], old[:, piece(c)]
            new[:, piece(c)] = before + (innov[:, piece(c)] - spread_of * before - seen) / spread_of
            return carry

        lax.fori_loop(0, obs // chunk, step, 0)

    def cover(source, target, s):
        high, low = split(source[s])
        smooth = dot(high, zonal_hi[...]) + (dot(high, zonal_lo[...]) + dot(low, zonal_hi[...]))
        high, low = split(smooth)
        mixed = smooth + (dot(mix_hi[...], high) + (dot(mix_hi[...], low) + dot(mix_lo[...], high)))
        target[s] = mixed

    def first(lev):
        for s in (0, 1):
            wind = traj[s, lev]
            east[s, lev] = 0.1 + 0.25 * jnp.tanh(wind)
            north[s, lev] = 0.1 + 0.25 * sine(wind)
            value = pull(0, s, lev, dual[s, lev])
            if s == 0:
                pull_send[0, lev] = value
            else:
                pulled[lev] = value
            edge_rows(2, s, lev, incr[s, lev])

    for name in ("dep", "table", "mix"):
        loads[name].start()
    for name in ("traj", "dual", "incr"):
        loads[name].wait()
    each_level(first)
    await_barrier()

    @pl.when(has_prev)
    def _():
        pull_copy(0).start()

    for s in (1, 0):
        halo_start(0, s)

    @pl.when(has_next)
    def _():
        prior_copy(0, incr).start()

    for s in (0, 1):
        halo_start(2, s)

    tables()
    spread(held)

    def response():
        modes = width // 2
        row = jnp.broadcast_to(spectrum_ref[pl.ds(0, modes)].reshape(1, modes), (ROWS, modes))
        high, low = split(row)
        table_hi, table_lo = split(table[...])
        first = dot(high, table_hi) + (dot(high, table_lo) + dot(low, table_hi))
        cell = lax.broadcasted_iota(jnp.int32, (ROWS, width), 1)
        parity = 1.0 - 2.0 * jnp.bitwise_and(cell, 1).astype(F32)
        first = first + parity * (spectrum_ref[pl.ds(modes, 1)].reshape(1, 1) * (1.0 / width))
        rows = first
        for step in range(1, ROWS):
            rows = jnp.where(line == step, pltpu.roll(first, step, 1), rows)
        return rows

    def circulant(rows, a, carry):
        tall = [pltpu.roll(rows, a * 16 + t, 1) for t in (0, 8)]
        high, low = split(jnp.concatenate(tall, axis=0))
        at = pl.ds(pl.multiple_of(a * 16, 16), 16)
        zonal_hi[at, :] = high
        zonal_lo[at, :] = low
        return carry

    halo_wait(0, 0)

    def dual1_here(lev):
        field = pulled[lev] + pulled_halo(0, 0, lev) - spread_ref[rows_of(lev), :]
        dual1[0, lev] = field
        pull_send[1, lev] = pull(1, 0, lev, field)

    each_level(dual1_here)

    @pl.when(has_prev)
    def _():
        pull_copy(1).start()

    halo_start(1, 0)
    send_out(dual1, fore1, 0, 0)
    for name in ("dep", "table", "mix"):
        loads[name].wait()
    lax.fori_loop(0, width // 16, functools.partial(circulant, response()), 0)
    mix_hi[...], mix_lo[...] = split(mix_ref[...])
    hear_next(pull_copy(0), pull_recv.at[0])
    halo_wait(0, 1)

    def dual1_next(lev):
        field = pull_recv[0, lev] + pulled_halo(0, 1, lev) - spread_ref[rows_of(levels + lev), :]
        dual1[1, lev] = field
        pulled[lev] = pull(1, 1, lev, field)

    each_level(dual1_next)
    halo_start(1, 1)
    send_out(dual1, fore1, 0, 1)

    observe(incr, held, held1)
    spread(held1)
    halo_wait(1, 0)

    def dual2_here(lev):
        out_dual[0, lev] = pulled[lev] + pulled_halo(1, 0, lev) - spread_ref[rows_of(lev), :]

    each_level(dual2_here)
    send_out(out_dual, fore2, 1, 0)
    hear_next(pull_copy(1), pull_recv.at[1])
    halo_wait(1, 1)

    def dual2_next(lev):
        out_dual[1, lev] = pull_recv[1, lev] + pulled_halo(1, 1, lev) - spread_ref[rows_of(levels + lev), :]

    each_level(dual2_next)
    dual_store = pltpu.make_async_copy(out_dual, dual_any_out, store_sem.at[0])
    dual_store.start()
    send_out(out_dual, fore2, 1, 1)

    for s in (1, 0):
        far_copy(dual1, fore1, 0, s).wait_recv()
        cover(fore1, mixed1, s)
        send_back(mixed1, back1, 2, s)

    hear_prev(prior_copy(0, incr), prior.at[0])
    halo_wait(2, 0)
    halo_wait(2, 1)

    def moved1(lev):
        part[0, lev] = dep[0, lev] + push(2, 0, lev, prior[0, lev])
        part[1, lev] = dep[1, lev] + push(2, 1, lev, incr[0, lev])

    each_level(moved1)

    def second_filter():
        for s in (1, 0):
            far_copy(out_dual, fore2, 1, s).wait_recv()
            cover(fore2, mixed2, s)
            send_back(mixed2, back2, 3, s)

    pl.when(grp <= groups // 2)(second_filter)

    for s in (1, 0):
        far_copy(mixed1, back1, 2, s).wait_recv()

        def incr1_of(lev, s=s):
            field = part[s, lev] - back1[s, lev] * (scale_ref[s] * scale_ref[s])
            incr1[s, lev] = field
            edge_rows(3, s, lev, field)

        each_level(incr1_of)
        if s == 1:

            @pl.when(has_next)
            def _():
                prior_copy(1, incr1).start()

        halo_start(3, s)

    observe(incr1, held1, out_held)
    pl.when(grp > groups // 2)(second_filter)

    def finish(s, lev, before):
        field = dep[s, lev] + push(3, s, lev, before) - back2[s, lev] * (scale_ref[s] * scale_ref[s])
        out_incr[s, lev] = field
        slid_send[s, lev] = traj[s, lev] + field

    def slid_copy(s):
        return remote(slid_send.at[s], slid_any_out.at[s], slid_ssem.at[s], slid_rsem.at[s], (grp - 1, me))

    def incr_store(s):
        return pltpu.make_async_copy(out_incr.at[s], incr_any_out.at[s], store_sem.at[1 + s])

    def stay(s):
        return pltpu.make_async_copy(slid_send.at[1], slid_any_out.at[s], store_sem.at[3 + s])

    for s in (1, 0):
        if s == 0:
            hear_prev(prior_copy(1, incr1), prior.at[1])
        halo_wait(3, s)
        far_copy(mixed2, back2, 3, s).wait_recv()
        each_level(lambda lev, s=s: finish(s, lev, prior[1, lev] if s == 0 else incr1[0, lev]))

        @pl.when(has_prev)
        def _(s=s):
            slid_copy(s).start()

        incr_store(s).start()

    @pl.when(jnp.logical_not(has_next))
    def _():
        for s in (0, 1):
            stay(s).start()
        for s in (0, 1):
            stay(s).wait()

    for s in (0, 1):

        @pl.when(has_next)
        def _(s=s):
            slid_copy(s).wait_recv()

    dual_store.wait()
    for s in (0, 1):
        incr_store(s).wait()
    for s in (0, 1):
        far_copy(dual1, fore1, 0, s).wait_send()
        far_copy(out_dual, fore2, 1, s).wait_send()
        far_copy(mixed1, back1, 2, s).wait_send()
        far_copy(mixed2, back2, 3, s).wait_send()
    for phase in range(4):
        for way in (0, 1):
            for s in (0, 1):

                @pl.when(halo_sends(phase, way, s))
                def _(phase=phase, way=way, s=s):
                    halo(phase, way, s).wait_send()

    @pl.when(has_prev)
    def _():
        pull_copy(0).wait_send()
        pull_copy(1).wait_send()
        slid_copy(0).wait_send()
        slid_copy(1).wait_send()

    @pl.when(has_next)
    def _():
        prior_copy(0, incr).wait_send()
        prior_copy(1, incr1).wait_send()


def cosine_table(width):
    modes, cells = np.arange(width // 2), np.arange(width)
    weight = np.where(modes == 0, 1.0, 2.0) / width
    angle = (modes[:, None] * cells[None, :] % width) * (2.0 * math.pi / width)
    return jnp.asarray((np.cos(angle) * weight[:, None]).astype(np.float32))


def hand_over(count, *refs):
    sources, targets, held = refs[:count], refs[count : 2 * count], refs[2 * count : 3 * count]
    load_sem, store_sem = refs[3 * count :]
    loads = [pltpu.make_async_copy(a, b, load_sem.at[i]) for i, (a, b) in enumerate(zip(sources, held))]
    stores = [pltpu.make_async_copy(a, b, store_sem.at[i]) for i, (a, b) in enumerate(zip(held, targets))]
    for load in loads:
        load.start()
    for load, store in zip(loads, stores):
        load.wait()
        store.start()
    for store in stores:
        store.wait()


def on_device(
    departures,
    innovations,
    obs_variance,
    dual_state,
    obs_dual,
    increment,
    trajectory,
    lat_mix,
    spectrum,
    error_scale,
    obs_time,
    obs_level,
    obs_point,
):
    groups, bands = lax.axis_size("tm"), lax.axis_size("space")
    windows, levels, rows, width = increment.shape
    lats = bands * rows
    obs = obs_dual.shape[0]
    cells = windows * levels * rows
    flat = [v.reshape(1, obs) for v in (innovations, obs_variance, obs_dual, obs_time, obs_level, obs_point)]
    state = jax.ShapeDtypeStruct(increment.shape, F32)
    held_shape = jax.ShapeDtypeStruct((1, obs), F32)
    vmem = pl.BlockSpec(memory_space=pltpu.VMEM)
    anywhere = pl.BlockSpec(memory_space=pl.ANY)
    whole = pltpu.VMEM(increment.shape, F32)
    pencil = pltpu.VMEM((windows, lats, width), F32)
    window = pltpu.VMEM((levels, rows, width), F32)
    window2 = pltpu.VMEM((2, levels, rows, width), F32)
    edge = pltpu.VMEM((4, 2, 2, levels, width), F32)
    dma = pltpu.SemaphoreType.DMA
    dual, held, incr, slid = pl.pallas_call(
        functools.partial(kernel, groups, bands),
        out_shape=(state, held_shape, state, state),
        in_specs=[pl.BlockSpec(memory_space=pltpu.SMEM)] + [anywhere] * 6 + [vmem] * 7,
        out_specs=(anywhere, vmem, anywhere, anywhere),
        scratch_shapes=[
            pltpu.VMEM((width // 2, width), F32),
            pltpu.VMEM((lats, lats), F32),
            whole,
            whole,
            whole,
            whole,
            whole,
            whole,
            whole,
            whole,
            pltpu.VMEM((width, width), BF16),
            pltpu.VMEM((width, width), BF16),
            pltpu.VMEM((lats, lats), BF16),
            pltpu.VMEM((lats, lats), BF16),
            pltpu.VMEM((1, obs), jnp.int32),
            pltpu.VMEM((1, obs), jnp.int32),
            pltpu.VMEM((cells, obs), BF16),
            pltpu.VMEM((cells, width), F32),
            pltpu.VMEM((width, cells), BF16),
            pltpu.VMEM((width, cells), BF16),
            pltpu.VMEM((1, obs), F32),
            whole,
            window,
            window2,
            window2,
            window2,
            whole,
            whole,
            whole,
            pencil,
            pencil,
            pencil,
            pencil,
            whole,
            whole,
            edge,
            edge,
            dma((4, 2)),
            dma((4, 2)),
            dma((2,)),
            dma((2,)),
            dma((2,)),
            dma((2,)),
            dma((2,)),
            dma((2,)),
            dma((4, 2, 2)),
            dma((4, 2, 2)),
            dma((6,)),
            dma((5,)),
        ],
        compiler_params=pltpu.CompilerParams(
            collective_id=0, has_side_effects=True, vmem_limit_bytes=56 * 1024 * 1024
        ),
    )(
        error_scale,
        cosine_table(width),
        lat_mix,
        departures,
        dual_state,
        increment,
        trajectory,
        spectrum,
        *flat,
    )
    memory = pl.BlockSpec(memory_space=pltpu.HBM)
    dual, held, incr, slid = pl.pallas_call(
        functools.partial(hand_over, 4),
        out_shape=(state, held_shape, state, state),
        in_specs=[memory] * 4,
        out_specs=(memory,) * 4,
        scratch_shapes=[whole, pltpu.VMEM((1, obs), F32), whole, whole, dma((4,)), dma((4,))],
    )(dual, held, incr, slid)
    return (dual, held.reshape(obs), incr, slid)


def solution(mesh):
    state = P("tm", None, "space", None)
    flat = P(("tm", "space"))
    placed = (state, flat, flat, state, flat, state, state, P(), P(), P("tm"), flat, flat, flat)
    return jax.shard_map(
        on_device,
        mesh=mesh,
        in_specs=placed,
        out_specs=(state, flat, state, state),
        check_vma=False,
    )
```

```python
import functools
import math

import jax
import jax.numpy as jnp
import numpy as np
from jax import lax
from jax.experimental import pallas as pl
from jax.experimental.pallas import tpu as pltpu
from jax.sharding import PartitionSpec as P

MESH = pl.DeviceIdType.MESH
ROWS = 8
GROUP = 4
F32 = jnp.float32
BF16 = jnp.bfloat16
SINE = (-2.5052108385e-8, 2.7557319224e-6, -1.9841269841e-4, 8.3333333333e-3, -1.6666666667e-1)


def sine(angle):
    turns = jnp.floor(angle * (1.0 / math.pi) + 0.5)
    rest = angle - turns * 3.140625
    rest = rest - turns * 9.67653589793e-4
    square = rest * rest
    series = SINE[0]
    for factor in SINE[1:]:
        series = series * square + factor
    half = turns * 0.5
    sign = 1.0 - 4.0 * (half - jnp.floor(half))
    return sign * (rest + rest * square * series)


def split(values):
    high = values.astype(BF16)
    return high, (values - high.astype(F32)).astype(BF16)


def dot(left, right, dims=((1,), (0,))):
    return lax.dot_general(left, right, (dims, ((), ())), preferred_element_type=F32)


def kernel(
    groups,
    bands,
    scale_ref,
    table_any,
    mix_any,
    dep_any,
    dual_any,
    incr_any,
    traj_any,
    spectrum_ref,
    innov,
    variance,
    held,
    time_ref,
    level_ref,
    point_ref,
    dual_any_out,
    out_held,
    incr_any_out,
    slid_any_out,
    table,
    mix_ref,
    dep,
    dual,
    incr,
    traj,
    out_dual,
    out_incr,
    east,
    north,
    zonal_hi,
    zonal_lo,
    mix_hi,
    mix_lo,
    row_ref,
    lon_ref,
    row_table,
    spread_ref,
    turned_hi,
    turned_lo,
    held1,
    dual1,
    pulled,
    pull_send,
    pull_recv,
    prior,
    incr1,
    part,
    slid_send,
    fore1,
    fore2,
    mixed1,
    mixed2,
    back1,
    back2,
    halo_send,
    halo_recv,
    far_send,
    far_recv,
    pull_ssem,
    pull_rsem,
    prior_ssem,
    prior_rsem,
    slid_ssem,
    slid_rsem,
    halo_ssem,
    halo_rsem,
    load_sem,
    store_sem,
):
    windows, levels, _, width = dep.shape
    obs = innov.shape[1]
    cells = windows * levels * ROWS
    chunk = min(2048, obs)
    me = lax.axis_index("space")
    grp = lax.axis_index("tm")
    has_prev, has_next = grp > 0, grp < groups - 1
    has_below, has_above = me > 0, me < bands - 1
    line = lax.broadcasted_iota(jnp.int32, (ROWS, width), 0)
    is_first, is_last = line == 0, line == ROWS - 1

    loads = {}
    for place, (name, source, target) in enumerate(
        (
            ("traj", traj_any, traj),
            ("dual", dual_any, dual),
            ("incr", incr_any, incr),
            ("dep", dep_any, dep),
            ("table", table_any, table),
            ("mix", mix_any, mix_ref),
        )
    ):
        loads[name] = pltpu.make_async_copy(source, target, load_sem.at[place])

    def both(*flags):
        return functools.reduce(jnp.logical_and, flags)

    for name in ("traj", "dual", "incr"):
        loads[name].start()

    barrier = pltpu.get_barrier_semaphore()
    around = ((0, None), (-1, has_below), (1, has_above))

    def greet(j, carry):
        pl.semaphore_signal(barrier, inc=1, device_id=(grp, lax.rem(me + j, bands)), device_id_type=MESH)
        return carry

    lax.fori_loop(1, bands, greet, 0)
    for shift, there in ((-1, has_prev), (1, has_next)):
        for step, beside in around:
            flags = [there] if beside is None else [there, beside]

            @pl.when(both(*flags))
            def _(shift=shift, step=step):
                pl.semaphore_signal(barrier, inc=1, device_id=(grp + shift, me + step), device_id_type=MESH)

    def await_barrier():
        beside = 1 + has_below.astype(jnp.int32) + has_above.astype(jnp.int32)
        other = has_prev.astype(jnp.int32) + has_next.astype(jnp.int32)
        pl.semaphore_wait(barrier, bands - 1 + other * beside)

    def remote(source, target, ssem, rsem, device):
        return pltpu.make_async_remote_copy(
            src_ref=source, dst_ref=target, send_sem=ssem, recv_sem=rsem, device_id=device, device_id_type=MESH
        )

    def each_level(body):
        def step(i, carry):
            for u in range(GROUP):
                body(i * GROUP + u)
            return carry

        lax.fori_loop(0, levels // GROUP, step, 0)

    def rows_of(j):
        return pl.ds(pl.multiple_of(j * ROWS, ROWS), ROWS)

    def send_out(source, target, k, s):
        def step(j, carry):
            to = lax.rem(me + j, bands)
            remote(source.at[s, to], target.at[s, rows_of(me)], far_send.at[k, s], far_recv.at[k, s], (grp, to)).start()
            return carry

        lax.fori_loop(1, bands, step, 0)
        target[s, rows_of(me), :] = source[s, me]

    def send_back(source, target, k, s):
        def step(j, carry):
            to = lax.rem(me + j, bands)
            remote(source.at[s, rows_of(to)], target.at[s, me], far_send.at[k, s], far_recv.at[k, s], (grp, to)).start()
            return carry

        lax.fori_loop(1, bands, step, 0)
        target[s, me] = source[s, rows_of(me), :]

    def all_but_one(ref, s):
        return ref.at[s, pl.ds(0, bands - 1)] if ref.ndim == 4 else ref.at[s, pl.ds(0, (bands - 1) * ROWS)]

    def far_copy(source, target, k, s):
        return remote(all_but_one(source, s), all_but_one(target, s), far_send.at[k, s], far_recv.at[k, s], (grp, me))

    def halo(phase, way, s):
        pulls = phase < 2
        to_group = (grp - 1 if pulls else grp) if s == 0 else (grp if pulls else grp + 1)
        to_band = me + 1 if way == 0 else me - 1
        return remote(
            halo_send.at[phase, way, s],
            halo_recv.at[phase, way, 1 - s],
            halo_ssem.at[phase, way, s],
            halo_rsem.at[phase, way, 1 - s],
            (to_group, to_band),
        )

    def halo_sends(phase, way, s):
        beside = has_above if way == 0 else has_below
        if phase < 2 and s == 0:
            return both(beside, has_prev)
        if phase >= 2 and s == 1:
            return both(beside, has_next)
        return beside

    def halo_hears(phase, way, s):
        beside = has_below if way == 0 else has_above
        if phase < 2 and s == 1:
            return both(beside, has_next)
        if phase >= 2 and s == 0:
            return both(beside, has_prev)
        return beside

    def halo_start(phase, s):
        for way in (0, 1):

            @pl.when(halo_sends(phase, way, s))
            def _(way=way):
                halo(phase, way, s).start()

    def halo_wait(phase, s):
        for way in (0, 1):

            @pl.when(halo_hears(phase, way, s))
            def _(way=way):
                halo(phase, way, 1 - s).wait_recv()

            @pl.when(jnp.logical_not(halo_hears(phase, way, s)))
            def _(way=way):
                halo_recv[phase, way, s] = jnp.zeros((levels, width), F32)

    def halo_row(phase, way, s, lev):
        return halo_recv[phase, way, s, pl.ds(lev, 1), :]

    def pull_copy(k):
        return remote(pull_send.at[k], pull_recv.at[k], pull_ssem.at[k], pull_rsem.at[k], (grp - 1, me))

    def prior_copy(k, source):
        return remote(source.at[1], prior.at[k], prior_ssem.at[k], prior_rsem.at[k], (grp + 1, me))

    def hear_next(copy, buffer):
        @pl.when(has_next)
        def _():
            copy.wait_recv()

        @pl.when(jnp.logical_not(has_next))
        def _():
            buffer[...] = jnp.zeros(buffer.shape, F32)

    def hear_prev(copy, buffer):
        @pl.when(has_prev)
        def _():
            copy.wait_recv()

        @pl.when(jnp.logical_not(has_prev))
        def _():
            buffer[...] = jnp.zeros(buffer.shape, F32)

    def pull(phase, s, lev, field):
        pe, pn = east[s, lev], north[s, lev]
        down = field * pn
        up = field * (0.2 - pn)
        halo_send[phase, 0, s, pl.ds(lev, 1), :] = up[ROWS - 1 :, :]
        halo_send[phase, 1, s, pl.ds(lev, 1), :] = down[:1, :]
        return (
            0.6 * field
            + pltpu.roll(field * pe, width - 1, 1)
            + pltpu.roll(field * (0.2 - pe), 1, 1)
            + jnp.where(is_last, 0.0, pltpu.roll(down, ROWS - 1, 0))
            + jnp.where(is_first, 0.0, pltpu.roll(up, 1, 0))
        )

    def pulled_halo(phase, s, lev):
        return jnp.where(is_first, halo_row(phase, 0, s, lev), 0.0) + jnp.where(is_last, halo_row(phase, 1, s, lev), 0.0)

    def push(phase, s, lev, field):
        pe, pn = east[s, lev], north[s, lev]
        above = jnp.where(is_last, halo_row(phase, 1, s, lev), pltpu.roll(field, ROWS - 1, 0))
        below = jnp.where(is_first, halo_row(phase, 0, s, lev), pltpu.roll(field, 1, 0))
        return (
            0.6 * field
            + pltpu.roll(field, width - 1, 1) * (0.2 - pe)
            + pltpu.roll(field, 1, 1) * pe
            + above * (0.2 - pn)
            + below * pn
        )

    def edge_rows(phase, s, lev, field):
        halo_send[phase, 0, s, pl.ds(lev, 1), :] = field[ROWS - 1 :, :]
        halo_send[phase, 1, s, pl.ds(lev, 1), :] = field[:1, :]

    def piece(c):
        return pl.ds(pl.multiple_of(c * chunk, chunk), chunk)

    def tables():
        shift = width.bit_length() - 1
        point = point_ref[...]
        row_ref[...] = ((time_ref[...] - grp * windows) * levels + level_ref[...]) * ROWS + (
            lax.shift_right_logical(point, shift) - me * ROWS
        )
        lon_ref[...] = jnp.bitwise_and(point, width - 1)

        def step(c, carry):
            wanted = row_ref[:, piece(c)]
            block = 64
            for r in range(0, cells, block):
                spot = lax.broadcasted_iota(jnp.int32, (block, chunk), 0) + r
                row_table[r : r + block, piece(c)] = jnp.where(spot == wanted, 1.0, 0.0).astype(BF16)
            return carry

        lax.fori_loop(0, obs // chunk, step, 0)

    def spread(values):
        spread_ref[...] = jnp.zeros(spread_ref.shape, F32)

        def step(c, carry):
            weight = values[:, piece(c)]
            high = weight.astype(BF16).astype(F32)
            low = weight - high
            hit = lax.broadcasted_iota(jnp.int32, (width, chunk), 0) == lon_ref[:, piece(c)]
            chosen = row_table[:, piece(c)]
            total = dot(chosen, jnp.where(hit, high, 0.0).astype(BF16), ((1,), (1,)))
            total = total + dot(chosen, jnp.where(hit, low, 0.0).astype(BF16), ((1,), (1,)))
            spread_ref[...] += total
            return carry

        lax.fori_loop(0, obs // chunk, step, 0)

    def observe(state, old, new):
        turned = state[...].reshape(cells, width).T
        turned_hi[...], turned_lo[...] = split(turned)

        def step(c, carry):
            chosen = row_table[:, piece(c)]
            picked = dot(turned_hi[...], chosen) + dot(turned_lo[...], chosen)
            hit = lax.broadcasted_iota(jnp.int32, (width, chunk), 0) == lon_ref[:, piece(c)]
            seen = jnp.sum(jnp.where(hit, picked, 0.0), axis=0, keepdims=True)
            spread_of, before = variance[:, piece(c)], old[:, piece(c)]
            new[:, piece(c)] = before + (innov[:, piece(c)] - spread_of * before - seen) / spread_of
            return carry

        lax.fori_loop(0, obs // chunk, step, 0)

    def cover(source, target, s):
        high, low = split(source[s])
        smooth = dot(high, zonal_hi[...]) + (dot(high, zonal_lo[...]) + dot(low, zonal_hi[...]))
        high, low = split(smooth)
        mixed = smooth + (dot(mix_hi[...], high) + (dot(mix_hi[...], low) + dot(mix_lo[...], high)))
        target[s] = mixed

    def first(lev):
        for s in (0, 1):
            wind = traj[s, lev]
            east[s, lev] = 0.1 + 0.25 * jnp.tanh(wind)
            north[s, lev] = 0.1 + 0.25 * sine(wind)
            value = pull(0, s, lev, dual[s, lev])
            if s == 0:
                pull_send[0, lev] = value
            else:
                pulled[lev] = value
            edge_rows(2, s, lev, incr[s, lev])

    for name in ("dep", "table", "mix"):
        loads[name].start()
    for name in ("traj", "dual", "incr"):
        loads[name].wait()
    each_level(first)
    await_barrier()

    @pl.when(has_prev)
    def _():
        pull_copy(0).start()

    for s in (1, 0):
        halo_start(0, s)

    @pl.when(has_next)
    def _():
        prior_copy(0, incr).start()

    for s in (0, 1):
        halo_start(2, s)

    tables()
    spread(held)

    def response():
        modes = width // 2
        row = jnp.broadcast_to(spectrum_ref[pl.ds(0, modes)].reshape(1, modes), (ROWS, modes))
        high, low = split(row)
        table_hi, table_lo = split(table[...])
        first = dot(high, table_hi) + (dot(high, table_lo) + dot(low, table_hi))
        cell = lax.broadcasted_iota(jnp.int32, (ROWS, width), 1)
        parity = 1.0 - 2.0 * jnp.bitwise_and(cell, 1).astype(F32)
        first = first + parity * (spectrum_ref[pl.ds(modes, 1)].reshape(1, 1) * (1.0 / width))
        rows = first
        for step in range(1, ROWS):
            rows = jnp.where(line == step, pltpu.roll(first, step, 1), rows)
        return rows

    def circulant(rows, a, carry):
        tall = [pltpu.roll(rows, a * 16 + t, 1) for t in (0, 8)]
        high, low = split(jnp.concatenate(tall, axis=0))
        at = pl.ds(pl.multiple_of(a * 16, 16), 16)
        zonal_hi[at, :] = high
        zonal_lo[at, :] = low
        return carry

    halo_wait(0, 0)

    def dual1_here(lev):
        field = pulled[lev] + pulled_halo(0, 0, lev) - spread_ref[rows_of(lev), :]
        dual1[0, lev] = field
        pull_send[1, lev] = pull(1, 0, lev, field)

    each_level(dual1_here)

    @pl.when(has_prev)
    def _():
        pull_copy(1).start()

    halo_start(1, 0)
    send_out(dual1, fore1, 0, 0)
    for name in ("dep", "table", "mix"):
        loads[name].wait()
    lax.fori_loop(0, width // 16, functools.partial(circulant, response()), 0)
    mix_hi[...], mix_lo[...] = split(mix_ref[...])
    hear_next(pull_copy(0), pull_recv.at[0])
    halo_wait(0, 1)

    def dual1_next(lev):
        field = pull_recv[0, lev] + pulled_halo(0, 1, lev) - spread_ref[rows_of(levels + lev), :]
        dual1[1, lev] = field
        pulled[lev] = pull(1, 1, lev, field)

    each_level(dual1_next)
    halo_start(1, 1)
    send_out(dual1, fore1, 0, 1)

    observe(incr, held, held1)
    spread(held1)
    halo_wait(1, 0)

    def dual2_here(lev):
        out_dual[0, lev] = pulled[lev] + pulled_halo(1, 0, lev) - spread_ref[rows_of(lev), :]

    each_level(dual2_here)
    send_out(out_dual, fore2, 1, 0)
    hear_next(pull_copy(1), pull_recv.at[1])
    halo_wait(1, 1)

    def dual2_next(lev):
        out_dual[1, lev] = pull_recv[1, lev] + pulled_halo(1, 1, lev) - spread_ref[rows_of(levels + lev), :]

    each_level(dual2_next)
    dual_store = pltpu.make_async_copy(out_dual, dual_any_out, store_sem.at[0])
    dual_store.start()
    send_out(out_dual, fore2, 1, 1)

    for s in (1, 0):
        far_copy(dual1, fore1, 0, s).wait_recv()
        cover(fore1, mixed1, s)
        send_back(mixed1, back1, 2, s)

    hear_prev(prior_copy(0, incr), prior.at[0])
    halo_wait(2, 0)
    halo_wait(2, 1)

    def moved1(lev):
        part[0, lev] = dep[0, lev] + push(2, 0, lev, prior[0, lev])
        part[1, lev] = dep[1, lev] + push(2, 1, lev, incr[0, lev])

    each_level(moved1)

    def second_filter():
        for s in (1, 0):
            far_copy(out_dual, fore2, 1, s).wait_recv()
            cover(fore2, mixed2, s)
            send_back(mixed2, back2, 3, s)

    pl.when(grp <= groups // 2)(second_filter)

    for s in (1, 0):
        far_copy(mixed1, back1, 2, s).wait_recv()

        def incr1_of(lev, s=s):
            field = part[s, lev] - back1[s, lev] * (scale_ref[s] * scale_ref[s])
            incr1[s, lev] = field
            edge_rows(3, s, lev, field)

        each_level(incr1_of)
        if s == 1:

            @pl.when(has_next)
            def _():
                prior_copy(1, incr1).start()

        halo_start(3, s)

    observe(incr1, held1, out_held)
    pl.when(grp > groups // 2)(second_filter)

    def moved2(s, lev, before):
        part[s, lev] = dep[s, lev] + push(3, s, lev, before)

    def finish(s, lev):
        field = part[s, lev] - back2[s, lev] * (scale_ref[s] * scale_ref[s])
        out_incr[s, lev] = field
        slid_send[s, lev] = traj[s, lev] + field

    def slid_copy(s):
        return remote(slid_send.at[s], slid_any_out.at[s], slid_ssem.at[s], slid_rsem.at[s], (grp - 1, me))

    def incr_store(s):
        return pltpu.make_async_copy(out_incr.at[s], incr_any_out.at[s], store_sem.at[1 + s])

    def stay(s):
        return pltpu.make_async_copy(slid_send.at[1], slid_any_out.at[s], store_sem.at[3 + s])

    halo_wait(3, 1)
    each_level(lambda lev: moved2(1, lev, incr1[0, lev]))
    for s in (1, 0):
        if s == 0:
            hear_prev(prior_copy(1, incr1), prior.at[1])
            halo_wait(3, 0)
            each_level(lambda lev: moved2(0, lev, prior[1, lev]))
        far_copy(mixed2, back2, 3, s).wait_recv()
        each_level(functools.partial(finish, s))

        @pl.when(has_prev)
        def _(s=s):
            slid_copy(s).start()

        incr_store(s).start()

    @pl.when(jnp.logical_not(has_next))
    def _():
        for s in (0, 1):
            stay(s).start()
        for s in (0, 1):
            stay(s).wait()

    for s in (0, 1):

        @pl.when(has_next)
        def _(s=s):
            slid_copy(s).wait_recv()

    dual_store.wait()
    for s in (0, 1):
        incr_store(s).wait()
    for s in (0, 1):
        far_copy(dual1, fore1, 0, s).wait_send()
        far_copy(out_dual, fore2, 1, s).wait_send()
        far_copy(mixed1, back1, 2, s).wait_send()
        far_copy(mixed2, back2, 3, s).wait_send()
    for phase in range(4):
        for way in (0, 1):
            for s in (0, 1):

                @pl.when(halo_sends(phase, way, s))
                def _(phase=phase, way=way, s=s):
                    halo(phase, way, s).wait_send()

    @pl.when(has_prev)
    def _():
        pull_copy(0).wait_send()
        pull_copy(1).wait_send()
        slid_copy(0).wait_send()
        slid_copy(1).wait_send()

    @pl.when(has_next)
    def _():
        prior_copy(0, incr).wait_send()
        prior_copy(1, incr1).wait_send()


def cosine_table(width):
    modes, cells = np.arange(width // 2), np.arange(width)
    weight = np.where(modes == 0, 1.0, 2.0) / width
    angle = (modes[:, None] * cells[None, :] % width) * (2.0 * math.pi / width)
    return jnp.asarray((np.cos(angle) * weight[:, None]).astype(np.float32))


def hand_over(count, *refs):
    sources, targets, held = refs[:count], refs[count : 2 * count], refs[2 * count : 3 * count]
    load_sem, store_sem = refs[3 * count :]
    loads = [pltpu.make_async_copy(a, b, load_sem.at[i]) for i, (a, b) in enumerate(zip(sources, held))]
    stores = [pltpu.make_async_copy(a, b, store_sem.at[i]) for i, (a, b) in enumerate(zip(held, targets))]
    for load in loads:
        load.start()
    for load, store in zip(loads, stores):
        load.wait()
        store.start()
    for store in stores:
        store.wait()


def on_device(
    departures,
    innovations,
    obs_variance,
    dual_state,
    obs_dual,
    increment,
    trajectory,
    lat_mix,
    spectrum,
    error_scale,
    obs_time,
    obs_level,
    obs_point,
):
    groups, bands = lax.axis_size("tm"), lax.axis_size("space")
    windows, levels, rows, width = increment.shape
    lats = bands * rows
    obs = obs_dual.shape[0]
    cells = windows * levels * rows
    flat = [v.reshape(1, obs) for v in (innovations, obs_variance, obs_dual, obs_time, obs_level, obs_point)]
    state = jax.ShapeDtypeStruct(increment.shape, F32)
    held_shape = jax.ShapeDtypeStruct((1, obs), F32)
    vmem = pl.BlockSpec(memory_space=pltpu.VMEM)
    anywhere = pl.BlockSpec(memory_space=pl.ANY)
    whole = pltpu.VMEM(increment.shape, F32)
    pencil = pltpu.VMEM((windows, lats, width), F32)
    window = pltpu.VMEM((levels, rows, width), F32)
    window2 = pltpu.VMEM((2, levels, rows, width), F32)
    edge = pltpu.VMEM((4, 2, 2, levels, width), F32)
    dma = pltpu.SemaphoreType.DMA
    dual, held, incr, slid = pl.pallas_call(
        functools.partial(kernel, groups, bands),
        out_shape=(state, held_shape, state, state),
        in_specs=[pl.BlockSpec(memory_space=pltpu.SMEM)] + [anywhere] * 6 + [vmem] * 7,
        out_specs=(anywhere, vmem, anywhere, anywhere),
        scratch_shapes=[
            pltpu.VMEM((width // 2, width), F32),
            pltpu.VMEM((lats, lats), F32),
            whole,
            whole,
            whole,
            whole,
            whole,
            whole,
            whole,
            whole,
            pltpu.VMEM((width, width), BF16),
            pltpu.VMEM((width, width), BF16),
            pltpu.VMEM((lats, lats), BF16),
            pltpu.VMEM((lats, lats), BF16),
            pltpu.VMEM((1, obs), jnp.int32),
            pltpu.VMEM((1, obs), jnp.int32),
            pltpu.VMEM((cells, obs), BF16),
            pltpu.VMEM((cells, width), F32),
            pltpu.VMEM((width, cells), BF16),
            pltpu.VMEM((width, cells), BF16),
            pltpu.VMEM((1, obs), F32),
            whole,
            window,
            window2,
            window2,
            window2,
            whole,
            whole,
            whole,
            pencil,
            pencil,
            pencil,
            pencil,
            whole,
            whole,
            edge,
            edge,
            dma((4, 2)),
            dma((4, 2)),
            dma((2,)),
            dma((2,)),
            dma((2,)),
            dma((2,)),
            dma((2,)),
            dma((2,)),
            dma((4, 2, 2)),
            dma((4, 2, 2)),
            dma((6,)),
            dma((5,)),
        ],
        compiler_params=pltpu.CompilerParams(
            collective_id=0, has_side_effects=True, vmem_limit_bytes=56 * 1024 * 1024
        ),
    )(
        error_scale,
        cosine_table(width),
        lat_mix,
        departures,
        dual_state,
        increment,
        trajectory,
        spectrum,
        *flat,
    )
    memory = pl.BlockSpec(memory_space=pltpu.HBM)
    dual, held, incr, slid = pl.pallas_call(
        functools.partial(hand_over, 4),
        out_shape=(state, held_shape, state, state),
        in_specs=[memory] * 4,
        out_specs=(memory,) * 4,
        scratch_shapes=[whole, pltpu.VMEM((1, obs), F32), whole, whole, dma((4,)), dma((4,))],
    )(dual, held, incr, slid)
    return (dual, held.reshape(obs), incr, slid)


def solution(mesh):
    state = P("tm", None, "space", None)
    flat = P(("tm", "space"))
    placed = (state, flat, flat, state, flat, state, state, P(), P(), P("tm"), flat, flat, flat)
    return jax.shard_map(
        on_device,
        mesh=mesh,
        in_specs=placed,
        out_specs=(state, flat, state, state),
        check_vma=False,
    )
```
